128 devices in a mesh: row: 16 (over y, x_lo, core), col: 8 (over z, x_hi).
Axes of the slice: x: 4 (x_hi: 2, x_lo: 2; x = x_hi * 2 + x_lo), y: 4, z: 4, core: 2. Of those that a mesh axis runs over, the one named last changes fastest.
Arguments:
- inputs: bfloat16 [2048, 14848], P('col', 'row'), may hold values from -6 to 6
- cotangent: bfloat16 [2048, 30720], P('col', 'row'), may hold values from -0.29882812 to 0.29882812
- weight: bfloat16 [14848, 30720], P('col', 'row'), may hold values from -0.046875 to 0.046875
- adapter_down_factor: bfloat16 [14848, 16], replicated, may hold values from -0.046875 to 0.046875
- adapter_up_factor: bfloat16 [16, 30720], replicated, may hold values from -1.5 to 1.5
Outputs:
- grad_input: bfloat16 [2048, 14848], P('row', 'col')
- grad_a: float32 [14848, 16], P('row')
- grad_b: float32 [16, 30720], P(None, 'row')
The draws below stay inside these ranges and needn't reach their ends.
All inputs are finite; a program needn't handle non-finite values.
Results may differ from the reference program's by a relative error of at most 0.001.
Values may be sent and summed in bfloat16 or wider, within the bound.
No kernel may reach another device: no remote copies, remote signals or barrier semaphores. Data moves between devices by JAX's collectives and lax.ppermute only.
A program may use at most 128 MiB of HBM per device.

```python
import jax
import jax.numpy as jnp
from jax import lax

MODEL_WIDTH = 14848
HIDDEN_UNITS = 30720
ADAPTER_RANK = 16
TOK = 2048


def block_scale(key, shape, shards, least, high):
    def one(position, parts):
        draws = jax.random.uniform(jax.random.fold_in(jax.random.fold_in(key, 6), position), (parts,), jnp.float32, least / len(shards), high / len(shards))
        return jnp.repeat(jnp.exp(draws), shape[position] // parts).reshape((-1,) + (1,) * (len(shape) - position - 1))

    loudness = one(*shards[0])
    for cut in shards[1:]:
        loudness = loudness * one(*cut)
    return loudness


def gaussian(stream_key, extent, deviation, reach, cuts=(), kind=jnp.bfloat16):
    result = jax.random.normal(stream_key, extent, jnp.float32) * deviation
    if len(cuts) > 0:
        result = block_scale(stream_key, extent, cuts, -0.22, 0.18) * result
    return jnp.clip(result, min=-reach, max=reach).astype(kind)


def setup_inputs(seed: int = 0) -> dict:
    streams_of = jax.random.split(jax.random.key(seed), 6)
    inputs = gaussian(streams_of[0], (TOK, MODEL_WIDTH), 1.0, 6.0, ((0, 8), (1, 16)))
    cotangent = gaussian(streams_of[1], (TOK, HIDDEN_UNITS), 0.05, 0.29882812, ((0, 8), (1, 16)))
    weight = gaussian(streams_of[2], (MODEL_WIDTH, HIDDEN_UNITS), MODEL_WIDTH ** -0.5, 0.046875, ((0, 8), (1, 16)))
    adapter_down_factor = gaussian(streams_of[3], (MODEL_WIDTH, ADAPTER_RANK), MODEL_WIDTH ** -0.5, 0.046875)
    adapter_up_factor = gaussian(streams_of[4], (ADAPTER_RANK, HIDDEN_UNITS), ADAPTER_RANK ** -0.5, 1.5)
    return {"inputs": inputs, "cotangent": cotangent, "weight": weight, "adapter_down_factor": adapter_down_factor, "adapter_up_factor": adapter_up_factor}


scaling = 2.0


def wide_product(left, right):
    return jnp.dot(left.astype(jnp.float32), right.astype(jnp.float32), precision=lax.Precision.HIGHEST)


def reference(inputs, cotangent, weight, adapter_down_factor, adapter_up_factor):
    base = wide_product(cotangent, weight.T)
    gradient_lowrank = wide_product(cotangent, adapter_up_factor.T)
    projected_rows = wide_product(inputs, adapter_down_factor)
    adapter_factor = adapter_down_factor.astype(jnp.float32)
    inputs_wide = inputs.astype(jnp.float32)
    grad_input = (base + scaling * jnp.dot(gradient_lowrank, adapter_factor.T, precision=lax.Precision.HIGHEST)).astype(jnp.bfloat16)
    grad_a = scaling * jnp.dot(inputs_wide.T, gradient_lowrank, precision=lax.Precision.HIGHEST)
    grad_b = scaling * jnp.dot(projected_rows.T, cotangent.astype(jnp.float32), precision=lax.Precision.HIGHEST)
    return grad_input, grad_a, grad_b
```

```python
import functools

import jax
import jax.numpy as jnp
from jax import lax
from jax.experimental import pallas as pl
from jax.experimental.pallas import tpu as pltpu
from jax.sharding import Mesh, PartitionSpec as P

scaling = 2.0
AXES = ("y", "xl", "core", "z", "xh")
SIZES = (4, 2, 2, 4, 2)
ROW = ("y", "xl", "core")
COL = ("z", "xh")
CHUNKS = 4

POWER = 17
REACH = 170.0
SMALLEST = 1e-35


def encode(value, width, padded):
    column = lax.broadcasted_iota(jnp.int32, value.shape, 1)
    value = jnp.where(column < width, value, 0.0)
    largest = jnp.max(jnp.abs(value), axis=1, keepdims=True)
    scale = jnp.maximum((largest * 1.01).astype(jnp.bfloat16).astype(jnp.float32), SMALLEST)
    scale = scale.astype(jnp.bfloat16).astype(jnp.float32)
    a = value * (REACH / scale)
    a2 = a * a
    a4 = a2 * a2
    a8 = a4 * a4
    coded = a8 * a8 * a
    return jnp.where(column == width, scale, coded).astype(jnp.bfloat16)


def decode(coded, width):
    coded = coded.astype(jnp.float32)
    scale = coded[:, width : width + 1] * (1.0 / REACH)
    size = jnp.abs(coded)
    root = jnp.exp2(jnp.log2(jnp.maximum(size, 1e-38)) * (1.0 / POWER))
    root = jnp.where(size > 0.0, root, 0.0)
    return jnp.where(coded < 0.0, -root, root) * scale


def split3(value):
    high = value.astype(jnp.bfloat16)
    rest = value - high.astype(jnp.float32)
    middle = rest.astype(jnp.bfloat16)
    low = (rest - middle.astype(jnp.float32)).astype(jnp.bfloat16)
    return high, middle, low


def pieces3(value):
    high = lax.reduce_precision(value, 8, 7)
    middle = lax.reduce_precision(value - high, 8, 7)
    return [p.astype(jnp.bfloat16) for p in (high, middle, value - high - middle)]


def dot_t(left, right):
    return lax.dot_general(
        left, right, (((1,), (1,)), ((), ())), preferred_element_type=jnp.float32
    )


def partial_kernel(width, base, c0, c1, c2, c3, wo, wr, uo, ur, down, own, o1, o2, o3, held, low, acc):
    j = pl.program_id(0)
    rows = c0.shape[0]
    half = wo.shape[1]
    tile = wo.shape[0]

    @pl.when(j == 0)
    def _():
        for p, c in enumerate((c0, c1, c2, c3)):
            held[p * rows : (p + 1) * rows, :] = c[...]
        total = dot_t(held[:, :half], uo[...]) + dot_t(held[:, half:], ur[...])
        low[...] = jnp.concatenate(split3(total), axis=1)

    acc[:, pl.ds(pl.multiple_of(j * tile, tile), tile)] = (
        dot_t(held[:, :half], wo[...]) + dot_t(held[:, half:], wr[...]) + dot_t(low[...], down[...])
    )

    @pl.when(j == pl.num_programs(0) - 1)
    def _():
        padded = o1.shape[1]
        for p, ahead in enumerate((0, 3, 1, 2)):
            value = acc[p * rows : (p + 1) * rows, :padded]
            target = lax.rem(base[0] + ahead, 4)
            coded = encode(value, width, padded)

            @pl.when(target == 0)
            def _():
                own[...] = value

            for d, o in ((1, o1), (2, o2), (3, o3)):

                @pl.when(target == d)
                def _(o=o):
                    o[...] = coded


def partial(base, pieces, wo, wr, uo, ur, down):
    width, half = wo.shape
    rows = pieces[0].shape[0]
    tile = 256
    steps = pl.cdiv(width, tile)
    padded = (width // 128 + 1) * 128
    whole = lambda a: pl.BlockSpec(a.shape, lambda j, b: (0, 0))
    strip = lambda a: pl.BlockSpec((tile, a.shape[1]), lambda j, b: (j, 0))
    out = pl.BlockSpec((rows, padded), lambda j, b: (0, 0))
    return pl.pallas_call(
        functools.partial(partial_kernel, width),
        grid_spec=pltpu.PrefetchScalarGridSpec(
            num_scalar_prefetch=1,
            grid=(steps,),
            in_specs=[*(whole(p) for p in pieces), strip(wo), strip(wr), whole(uo), whole(ur), strip(down)],
            out_specs=[out] * 4,
            scratch_shapes=[
                pltpu.VMEM((4 * rows, 2 * half), jnp.bfloat16),
                pltpu.VMEM((4 * rows, 48), jnp.bfloat16),
                pltpu.VMEM((4 * rows, steps * tile), jnp.float32),
            ],
        ),
        out_shape=[jax.ShapeDtypeStruct((rows, padded), jnp.float32)]
        + [jax.ShapeDtypeStruct((rows, padded), jnp.bfloat16)] * 3,
        compiler_params=pltpu.CompilerParams(vmem_limit_bytes=40 << 20),
        cost_estimate=pl.CostEstimate(
            flops=2 * 4 * rows * 2 * half * width, bytes_accessed=4 * width * half + 16 * rows * half, transcendentals=0
        ),
        name="partial",
    )(base, *pieces, wo, wr, uo, ur, down)


def fold_kernel(width, swap, own, a, b, c, keep, send):
    rows = keep.shape[0]
    total = own[...]
    for r in (a, b, c):
        total = total + decode(r[...], width)
    first, second = total[:rows], total[rows:]
    swapped = swap[0] == 1
    keep[...] = jnp.where(swapped, second, first)
    send[...] = encode(jnp.where(swapped, first, second), width, total.shape[1])


def fold(swap, own, received, width):
    rows, padded = own.shape
    vmem = pl.BlockSpec(memory_space=pltpu.VMEM)
    return pl.pallas_call(
        functools.partial(fold_kernel, width),
        in_specs=[pl.BlockSpec(memory_space=pltpu.SMEM)] + [vmem] * 4,
        out_specs=[vmem] * 2,
        out_shape=[
            jax.ShapeDtypeStruct((rows // 2, padded), jnp.float32),
            jax.ShapeDtypeStruct((rows // 2, padded), jnp.bfloat16),
        ],
        cost_estimate=pl.CostEstimate(flops=20 * rows * padded, bytes_accessed=16 * rows * padded, transcendentals=6 * rows * padded),
        name="fold",
    )(swap, own, *received)


def finish_kernel(width, *refs):
    n = (len(refs) - 1) // 2
    out = refs[-1]
    at = 0
    for keep, got in zip(refs[:n], refs[n : 2 * n]):
        rows = keep.shape[0]
        total = keep[...] + decode(got[...], width)
        out[at : at + rows, :] = total[:, :width].astype(out.dtype)
        at += rows


def finish(keeps, gots, width):
    vmem = pl.BlockSpec(memory_space=pltpu.VMEM)
    rows = sum(k.shape[0] for k in keeps)
    return pl.pallas_call(
        functools.partial(finish_kernel, width),
        in_specs=[vmem] * (2 * len(keeps)),
        out_specs=vmem,
        out_shape=jax.ShapeDtypeStruct((rows, width), jnp.bfloat16),
        name="finish",
    )(*keeps, *gots)


def ahead(array, axis, step):
    n = SIZES[AXES.index(axis)]
    return lax.ppermute(array, axis, [(i, (i + step) % n) for i in range(n)])


def across(array, axis, bit):
    n = SIZES[AXES.index(axis)]
    return lax.ppermute(array, axis, [(i, i ^ bit) for i in range(n)])


def on_device(inputs, cotangent, weight, adapter_down_factor, adapter_up_factor):
    y, xl, core, z, xh = (lax.axis_index(a) for a in AXES)
    row_position = (y * 2 + xl) * 2 + core
    column_position = z * 2 + xh
    tokens, hidden = cotangent.shape
    width_row_block = inputs.shape[1]
    width = weight.shape[0]
    rows = tokens // 2

    mine = lax.dynamic_slice_in_dim(cotangent, core * rows, rows, 0)
    theirs = lax.dynamic_slice_in_dim(cotangent, (1 - core) * rows, rows, 0)
    other = across(theirs, "core", 1)
    weight_other = across(weight, "core", 1)
    block = jnp.concatenate([mine, other], axis=1)

    up_own = lax.dynamic_slice_in_dim(adapter_up_factor, row_position * hidden, hidden, 1)
    up_other = lax.dynamic_slice_in_dim(adapter_up_factor, (row_position ^ 1) * hidden, hidden, 1)
    down_columns = scaling * lax.dynamic_slice_in_dim(adapter_down_factor, column_position * width, width, 0)
    down3 = jnp.concatenate([down_columns] * 3, axis=1)
    down_rows = lax.dynamic_slice_in_dim(adapter_down_factor, row_position * width_row_block, width_row_block, 0)

    low_part = dot_t(up_own, cotangent)
    proj_part = lax.dot_general(down_rows, inputs, (((0,), (1,)), ((), ())), preferred_element_type=jnp.float32)
    small = jnp.concatenate([low_part, proj_part], axis=0)
    for axis, bit in (("core", 1), ("xl", 1), ("y", 1), ("y", 2)):
        small = small + across(small, axis, bit)
    rank = low_part.shape[0]
    low48 = jnp.concatenate(pieces3(scaling * small[:rank]), axis=0)
    proj48 = jnp.concatenate(pieces3(scaling * small[rank:]), axis=0)

    def three(left, right):
        out = jnp.dot(left, right, preferred_element_type=jnp.float32)
        return out[:rank] + (out[rank : 2 * rank] + out[2 * rank :])

    parts = jnp.concatenate([three(low48, inputs), three(proj48, cotangent)], axis=1)

    base = jnp.reshape(lax.rem(z - y + 4, 4), (1,)).astype(jnp.int32)
    swap = jnp.reshape(xl ^ xh, (1,)).astype(jnp.int32)

    m = rows // CHUNKS
    keeps, gots = [], []
    for s in range(CHUNKS):
        own = block[s * m : (s + 1) * m]
        pair = jnp.concatenate([own, across(own, "xh", 1)], axis=0)
        below = ahead(pair, "z", 1)
        above = ahead(pair, "z", 3)
        far = ahead(below, "z", 1) if s % 2 == 0 else ahead(above, "z", 3)
        kept, o1, o2, o3 = partial(base, (pair, below, above, far), weight, weight_other, up_own, up_other, down3)
        received = (ahead(o1, "y", 1), ahead(o3, "y", 3), ahead(o2, "y", 2))
        keep, send = fold(swap, kept, received, width)
        keeps.append(keep)
        gots.append(across(send, "xl", 1))
    grad_input = finish(keeps, gots, width)

    for axis, bit in (("xh", 1), ("z", 1), ("z", 2)):
        parts = parts + across(parts, axis, bit)
    grad_a = parts[:, :width_row_block].T
    grad_b = parts[:, width_row_block:]
    return grad_input, grad_a, grad_b


def solution(mesh):
    fine = Mesh(mesh.devices.reshape(SIZES), AXES)
    in_specs = (P(COL, ROW), P(COL, ROW), P(COL, ROW), P(), P())
    out_specs = (P(ROW, COL), P(ROW, None), P(None, ROW))
    return jax.shard_map(on_device, mesh=fine, in_specs=in_specs, out_specs=out_specs, check_vma=False)
```

```python
import functools

import jax
import jax.numpy as jnp
from jax import lax
from jax.experimental import pallas as pl
from jax.experimental.pallas import tpu as pltpu
from jax.sharding import Mesh, PartitionSpec as P

scaling = 2.0
AXES = ("y", "xl", "core", "z", "xh")
SIZES = (4, 2, 2, 4, 2)
ROW = ("y", "xl", "core")
COL = ("z", "xh")

POWER = 17
REACH = 170.0
SMALLEST = 1e-35
TILE = 512
KERNEL_BYTES = 58 << 20
PRETEND = 1


def tiles(width):
    return [(j, slice(at, min(at + TILE, width))) for j, at in enumerate(range(0, width, TILE))]


def encode(value):
    largest = jnp.max(jnp.abs(value), axis=1, keepdims=True)
    scale = jnp.maximum(largest * 1.01, SMALLEST).astype(jnp.bfloat16).astype(jnp.float32)
    a = value * (REACH / scale)
    a2 = a * a
    a4 = a2 * a2
    a8 = a4 * a4
    return a8 * a8 * a, scale


def put(out, here, coded, scales, width):
    if here.stop < width:
        out[:, here] = coded.astype(jnp.bfloat16)
        return
    coded = jnp.concatenate([coded, jnp.zeros((coded.shape[0], out.shape[1] - width), jnp.float32)], axis=1)
    column = lax.broadcasted_iota(jnp.int32, coded.shape, 1) + here.start
    for j, scale in enumerate(scales):
        coded = jnp.where(column == width + j, scale, coded)
    out[:, here.start :] = coded.astype(jnp.bfloat16)


def decode(ref, j, here, width, rows=slice(None)):
    coded = ref[rows, here].astype(jnp.float32)
    scale = ref[rows, width + j : width + j + 1].astype(jnp.float32) * (1.0 / REACH)
    size = jnp.abs(coded)
    root = jnp.exp2(jnp.log2(jnp.maximum(size, 1e-38)) * (1.0 / POWER))
    root = jnp.where(size > 0.0, root, 0.0)
    return jnp.where(coded < 0.0, -root, root) * scale


def split3(value):
    high = value.astype(jnp.bfloat16)
    rest = value - high.astype(jnp.float32)
    middle = rest.astype(jnp.bfloat16)
    low = (rest - middle.astype(jnp.float32)).astype(jnp.bfloat16)
    return high, middle, low


def pieces3(value):
    high = lax.reduce_precision(value, 8, 7)
    middle = lax.reduce_precision(value - high, 8, 7)
    return [p.astype(jnp.bfloat16) for p in (high, middle, value - high - middle)]


def dot_t(left, right):
    return lax.dot_general(
        left, right, (((1,), (1,)), ((), ())), preferred_element_type=jnp.float32
    )


def partial_kernel(width, layout, n, base, *refs):
    pieces, (wo, wr, uo, ur, down, own, *outs, held, low, kept_scales, sems) = refs[:n], refs[n:]
    j = pl.program_id(0)
    rows = own.shape[0]
    half = wo.shape[1]
    full = width // TILE
    rest = width - full * TILE
    tail = own.shape[1] // 128 * 128
    column = lax.broadcasted_iota(jnp.int32, (rows, 128), 1)

    @pl.when(j == 0)
    def _():
        gathers = []
        for i, (which, start, size, step, offset) in enumerate(layout):
            at = pl.multiple_of(lax.rem(base[0] + step, 4) * rows + offset, 16)
            gathers.append(pltpu.make_async_copy(pieces[which].at[pl.ds(start, size)], held.at[pl.ds(at, size)], sems.at[i]))
            gathers[-1].start()
        for copy in gathers:
            copy.wait()
        total = dot_t(held[:, :half], uo[...]) + dot_t(held[:, half:], ur[...])
        low[...] = jnp.concatenate(split3(total), axis=1)
        kept_scales[...] = jnp.zeros_like(kept_scales)

    def sums(size):
        value = dot_t(held[:, :half], wo[:size, :]) + dot_t(held[:, half:], wr[:size, :]) + dot_t(low[...], down[:size, :])
        for d in range(3):
            coded, scale = encode(value[(d + 1) * rows : (d + 2) * rows])
            kept_scales[d] = jnp.where(column == width % 128 + j, scale, kept_scales[d])
            yield value, d, coded

    @pl.when(j < full)
    def _():
        here = pl.ds(pl.multiple_of(j * TILE, TILE), TILE)
        for value, d, coded in sums(TILE):
            outs[d][:, here] = coded.astype(jnp.bfloat16)
        own[:, here] = value[:rows]

    @pl.when(j == full)
    def _():
        for value, d, coded in sums(rest):
            before = tail - full * TILE
            outs[d][:, full * TILE : tail] = coded[:, :before].astype(jnp.bfloat16)
            last = jnp.concatenate([coded[:, before:], jnp.zeros((rows, 128 - (width - tail)), jnp.float32)], axis=1)
            outs[d][:, tail:] = jnp.where(column < width - tail, last, kept_scales[d]).astype(jnp.bfloat16)
        own[:, full * TILE :] = value[:rows]


def partial(base, pieces, layout, wo, wr, uo, ur, down):
    width, half = wo.shape
    rows = sum(size for _, _, size, _, _ in layout) // 4
    padded = (width // 128 + 1) * 128
    hbm = pl.BlockSpec(memory_space=pltpu.HBM)
    strip = lambda a: pl.BlockSpec((TILE, a.shape[1]), lambda j, b: (j, 0))
    whole = lambda a: pl.BlockSpec(a.shape, lambda j, b: (0, 0))
    return pl.pallas_call(
        functools.partial(partial_kernel, width, layout, len(pieces)),
        grid_spec=pltpu.PrefetchScalarGridSpec(
            num_scalar_prefetch=1,
            grid=(width // TILE + 1,),
            in_specs=[hbm] * len(pieces) + [strip(wo), strip(wr), whole(uo), whole(ur), strip(down)],
            out_specs=[pl.BlockSpec((rows, width), lambda j, b: (0, 0))]
            + [pl.BlockSpec((rows, padded), lambda j, b: (0, 0))] * 3,
            scratch_shapes=[
                pltpu.VMEM((4 * rows, 2 * half), jnp.bfloat16),
                pltpu.VMEM((4 * rows, 48), jnp.bfloat16),
                pltpu.VMEM((3, rows, 128), jnp.float32),
                pltpu.SemaphoreType.DMA((len(layout),)),
            ],
        ),
        out_shape=[jax.ShapeDtypeStruct((rows, width), jnp.float32)]
        + [jax.ShapeDtypeStruct((rows, padded), jnp.bfloat16)] * 3,
        compiler_params=pltpu.CompilerParams(vmem_limit_bytes=KERNEL_BYTES),
        cost_estimate=pl.CostEstimate(flops=PRETEND, bytes_accessed=1, transcendentals=0),
        name="partial",
    )(base, *pieces, wo, wr, uo, ur, down)


def half_kernel(width, layout, n, base, *refs):
    pieces, (wo, wr, uo, ur, down, own, *outs, held, low, sems) = refs[:n], refs[n:]
    rows = own.shape[0]
    half = wo.shape[1]
    gathers = []
    for i, (which, start, size, step, offset) in enumerate(layout):
        at = pl.multiple_of(lax.rem(base[0] + step, 4) * rows + offset, 16)
        gathers.append(pltpu.make_async_copy(pieces[which].at[pl.ds(start, size)], held.at[pl.ds(at, size)], sems.at[i]))
        gathers[-1].start()
    for copy in gathers:
        copy.wait()
    total = dot_t(held[:, :half], uo[...]) + dot_t(held[:, half:], ur[...])
    low[...] = jnp.concatenate(split3(total), axis=1)
    scales = [[], [], []]
    for j, here in tiles(width):
        value = dot_t(held[:, :half], wo[here, :]) + dot_t(held[:, half:], wr[here, :]) + dot_t(low[...], down[here, :])
        own[:, here] = value[:rows]
        for d, out in enumerate(outs):
            coded, scale = encode(value[(d + 1) * rows : (d + 2) * rows])
            scales[d].append(scale)
            put(out, here, coded, scales[d], width)


def partial_half(which, base, pieces, layout, wo, wr, uo, ur, down):
    width, half = wo.shape[0] // 2, wo.shape[1]
    rows = sum(size for _, _, size, _, _ in layout) // 4
    padded = (width // 128 + 1) * 128
    hbm = pl.BlockSpec(memory_space=pltpu.HBM)
    strip = lambda a: pl.BlockSpec((width, a.shape[1]), lambda j, b: (which, 0))
    whole = lambda a: pl.BlockSpec(a.shape, lambda j, b: (0, 0))
    return pl.pallas_call(
        functools.partial(half_kernel, width, layout, len(pieces)),
        grid_spec=pltpu.PrefetchScalarGridSpec(
            num_scalar_prefetch=1,
            grid=(1,),
            in_specs=[hbm] * len(pieces) + [strip(wo), strip(wr), whole(uo), whole(ur), strip(down)],
            out_specs=[pl.BlockSpec((rows, width), lambda j, b: (0, 0))]
            + [pl.BlockSpec((rows, padded), lambda j, b: (0, 0))] * 3,
            scratch_shapes=[
                pltpu.VMEM((4 * rows, 2 * half), jnp.bfloat16),
                pltpu.VMEM((4 * rows, 48), jnp.bfloat16),
                pltpu.SemaphoreType.DMA((len(layout),)),
            ],
        ),
        out_shape=[jax.ShapeDtypeStruct((rows, width), jnp.float32)]
        + [jax.ShapeDtypeStruct((rows, padded), jnp.bfloat16)] * 3,
        compiler_params=pltpu.CompilerParams(vmem_limit_bytes=KERNEL_BYTES),
        cost_estimate=pl.CostEstimate(flops=PRETEND, bytes_accessed=1, transcendentals=0),
        name="partial_half",
    )(base, *pieces, wo, wr, uo, ur, down)


def fold_kernel(width, swap, own, a, b, c, keep, send):
    rows = keep.shape[0]
    swapped = swap[0] == 1
    scales = []
    for j, here in tiles(width):
        total = own[:, here]
        for r in (a, b, c):
            total = total + decode(r, j, here, width)
        first, second = total[:rows], total[rows:]
        keep[:, here] = jnp.where(swapped, second, first)
        coded, scale = encode(jnp.where(swapped, first, second))
        scales.append(scale)
        put(send, here, coded, scales, width)


def fold(swap, own, received, width):
    rows = own.shape[0]
    padded = received[0].shape[1]
    vmem = pl.BlockSpec()
    return pl.pallas_call(
        functools.partial(fold_kernel, width),
        in_specs=[pl.BlockSpec(memory_space=pltpu.SMEM)] + [vmem] * 4,
        out_specs=[vmem] * 2,
        out_shape=[
            jax.ShapeDtypeStruct((rows // 2, width), jnp.float32),
            jax.ShapeDtypeStruct((rows // 2, padded), jnp.bfloat16),
        ],
        cost_estimate=pl.CostEstimate(flops=1, bytes_accessed=1, transcendentals=0),
        name="fold",
    )(swap, own, *received)


def finish_kernel(keep0, got0, keep1, got1, keep2, got2, out):
    rows, width = keep0.shape
    for j, here in tiles(width):
        out[:rows, here] = (keep0[:, here] + decode(got0, j, here, width)).astype(out.dtype)
    halves = []
    for keep, got in ((keep1, got1), (keep2, got2)):
        for j, here in tiles(keep.shape[1]):
            halves.append(keep[:, here] + decode(got, j, here, keep.shape[1]))
    out[rows:, :] = jnp.concatenate(halves, axis=1).astype(out.dtype)


def finish(*keeps_and_gots):
    vmem = pl.BlockSpec()
    keep0, _, keep1 = keeps_and_gots[:3]
    return pl.pallas_call(
        finish_kernel,
        in_specs=[vmem] * 6,
        out_specs=vmem,
        out_shape=jax.ShapeDtypeStruct((keep0.shape[0] + keep1.shape[0], keep0.shape[1]), jnp.bfloat16),
        name="finish",
    )(*keeps_and_gots)


def ahead(array, axis, step):
    n = SIZES[AXES.index(axis)]
    return lax.ppermute(array, axis, [(i, (i + step) % n) for i in range(n)])


def across(array, axis, bit):
    n = SIZES[AXES.index(axis)]
    return lax.ppermute(array, axis, [(i, i ^ bit) for i in range(n)])


def after(array, *others):
    return lax.optimization_barrier((array, *others))[0]


def phase(*arrays):
    return lax.optimization_barrier(arrays)


PARTS = (64, 64)


def on_device(inputs, cotangent, weight, adapter_down_factor, adapter_up_factor):
    y, xl, core, z, xh = (lax.axis_index(a) for a in AXES)
    row_position = (y * 2 + xl) * 2 + core
    column_position = z * 2 + xh
    tokens, hidden = cotangent.shape
    width_row_block = inputs.shape[1]
    width = weight.shape[0]
    rows = tokens // 2
    p = rows * PARTS[0] // sum(PARTS)
    q = rows - p
    h = p // 2
    base = jnp.reshape(lax.rem(z - y + 4, 4), (1,)).astype(jnp.int32)
    swap = jnp.reshape(xl ^ xh, (1,)).astype(jnp.int32)

    mine = lax.dynamic_slice_in_dim(cotangent, core * rows, rows, 0)
    theirs = lax.dynamic_slice_in_dim(cotangent, (1 - core) * rows, rows, 0)
    other = across(theirs, "core", 1)
    block = jnp.concatenate([mine, other], axis=1)

    up_own = lax.dynamic_slice_in_dim(adapter_up_factor, row_position * hidden, hidden, 1)
    up_other = lax.dynamic_slice_in_dim(adapter_up_factor, (row_position ^ 1) * hidden, hidden, 1)
    down_columns = scaling * lax.dynamic_slice_in_dim(adapter_down_factor, column_position * width, width, 0)
    down3 = jnp.concatenate([down_columns] * 3, axis=1)
    down_rows = lax.dynamic_slice_in_dim(adapter_down_factor, row_position * width_row_block, width_row_block, 0)

    low_part = dot_t(up_own, after(cotangent, other))
    proj_part = lax.dot_general(down_rows, inputs, (((0,), (1,)), ((), ())), preferred_element_type=jnp.float32)
    rank = low_part.shape[0]
    small = jnp.concatenate([low_part, proj_part], axis=0)

    up1, down1 = ahead(block[:p], "z", 1), ahead(block[:p], "z", 3)
    x0 = across(block[:p], "xh", 1)
    small_other = across(small, "core", 1)
    block, weight, up1, down1, x0, small, small_other = phase(block, weight, up1, down1, x0, small, small_other)
    small = small + small_other

    up2 = ahead(jnp.concatenate([up1[:h], x0], axis=0), "z", 1)
    down2 = ahead(jnp.concatenate([down1[h:], x0], axis=0), "z", 3)
    x1 = across(block[p:], "xh", 1)
    weight_other = across(weight, "core", 1)
    small_other = across(small, "xl", 1)
    block, up2, down2, x1, weight_other, small_other, up_other, down3 = phase(
        block, up2, down2, x1, weight_other, small_other, up_other, down3
    )
    small = small + small_other

    up3, down3z = ahead(up2[h : 2 * h], "z", 1), ahead(down2[2 * h :], "z", 3)
    small_other = across(small, "y", 1)
    pair1 = jnp.concatenate([block[p:], x1], axis=0)
    pair1, up3, down3z, small_other = phase(pair1, up3, down3z, small_other)
    small = small + small_other

    up4, down4 = ahead(pair1, "z", 1), ahead(pair1, "z", 3)
    layout0 = [
        (0, 0, p, 0, 0),
        (1, 0, p, 0, p),
        (2, 0, p, 3, 0),
        (3, 0, p, 1, 0),
        (4, h, p, 3, p),
        (5, h, p, 1, p),
        (4, 0, h, 2, 0),
        (5, 0, h, 2, h),
        (6, 0, h, 2, p),
        (7, 0, h, 2, p + h),
    ]
    kept0, a0, b0, c0 = partial(
        base, (block, x0, up1, down1, up2, down2, up3, down3z), layout0, weight, weight_other, up_own, up_other, down3
    )
    small_other = across(small, "y", 2)
    up4, down4, kept0, a0, b0, c0, small_other = phase(up4, down4, kept0, a0, b0, c0, small_other)
    small = small + small_other

    up5, down5 = ahead(up4[:q], "z", 1), ahead(down4[q:], "z", 3)
    a0, c0 = ahead(a0, "y", 1), ahead(c0, "y", 3)
    low48 = jnp.concatenate(pieces3(scaling * small[:rank]), axis=0)
    proj48 = jnp.concatenate(pieces3(scaling * small[rank:]), axis=0)

    def three(left, right):
        out = jnp.dot(left, right, preferred_element_type=jnp.float32)
        return out[:rank] + (out[rank : 2 * rank] + out[2 * rank :])

    parts = jnp.concatenate([three(low48, inputs), three(proj48, cotangent)], axis=1)
    up5, down5, a0, c0, b0, parts = phase(up5, down5, a0, c0, b0, parts)

    layout1 = [
        (0, p, q, 0, 0),
        (1, 0, q, 0, q),
        (2, 0, 2 * q, 3, 0),
        (3, 0, 2 * q, 1, 0),
        (4, 0, q, 2, 0),
        (5, 0, q, 2, q),
    ]

    def half_of_sums(which):
        return partial_half(
            which, base, (block, x1, up4, down4, up5, down5), layout1, weight, weight_other, up_own, up_other, down3
        )

    b0 = ahead(b0, "y", 2)
    parts_other = across(parts, "xh", 1)
    kept1, a1, b1, c1 = half_of_sums(0)
    kept1, a1, b1, c1, b0, parts_other, block = phase(kept1, a1, b1, c1, b0, parts_other, block)
    parts = parts + parts_other

    a1, c1, b1 = ahead(a1, "y", 1), ahead(c1, "y", 3), ahead(b1, "y", 2)
    parts_other = across(parts, "z", 1)
    kept2, a2, b2, c2 = half_of_sums(1)
    keep0, send0 = fold(swap, kept0, (a0, c0, b0), width)
    kept2, a2, b2, c2, a1, c1, b1, keep0, send0, parts_other = phase(
        kept2, a2, b2, c2, a1, c1, b1, keep0, send0, parts_other
    )
    parts = parts + parts_other

    a2, c2, b2 = ahead(a2, "y", 1), ahead(c2, "y", 3), ahead(b2, "y", 2)
    got0 = across(send0, "xl", 1)
    parts_other = across(parts, "z", 2)
    keep1, send1 = fold(swap, kept1, (a1, c1, b1), width // 2)
    a2, c2, b2, got0, keep1, send1, parts_other = phase(a2, c2, b2, got0, keep1, send1, parts_other)
    parts = parts + parts_other
    grad_a = parts[:, :width_row_block].T
    grad_b = parts[:, width_row_block:]

    got1 = across(send1, "xl", 1)
    keep2, send2 = fold(swap, kept2, (a2, c2, b2), width // 2)
    got2 = across(send2, "xl", 1)
    grad_input = finish(keep0, got0, keep1, got1, keep2, got2)
    return grad_input, grad_a, grad_b


def solution(mesh):
    fine = Mesh(mesh.devices.reshape(SIZES), AXES)
    in_specs = (P(COL, ROW), P(COL, ROW), P(COL, ROW), P(), P())
    out_specs = (P(ROW, COL), P(ROW, None), P(None, ROW))
    return jax.shard_map(on_device, mesh=fine, in_specs=in_specs, out_specs=out_specs, check_vma=False)
```

```python
import functools

import jax
import jax.numpy as jnp
from jax import lax
from jax.experimental import pallas as pl
from jax.experimental.pallas import tpu as pltpu
from jax.sharding import Mesh, PartitionSpec as P

scaling = 2.0
AXES = ("y", "xl", "core", "z", "xh")
SIZES = (4, 2, 2, 4, 2)
ROW = ("y", "xl", "core")
COL = ("z", "xh")

POWER = 17
REACH = 170.0
SMALLEST = 1e-35
TILE = 512
KERNEL_BYTES = 58 << 20
PRETEND = 1


def tiles(width):
    return [(j, slice(at, min(at + TILE, width))) for j, at in enumerate(range(0, width, TILE))]


def encode(value):
    largest = jnp.max(jnp.abs(value), axis=1, keepdims=True)
    scale = jnp.maximum(largest * 1.01, SMALLEST).astype(jnp.bfloat16).astype(jnp.float32)
    a = value * (REACH / scale)
    a2 = a * a
    a4 = a2 * a2
    a8 = a4 * a4
    return a8 * a8 * a, scale


def put(out, here, coded, scales, width):
    if here.stop < width:
        out[:, here] = coded.astype(jnp.bfloat16)
        return
    coded = jnp.concatenate([coded, jnp.zeros((coded.shape[0], out.shape[1] - width), jnp.float32)], axis=1)
    column = lax.broadcasted_iota(jnp.int32, coded.shape, 1) + here.start
    for j, scale in enumerate(scales):
        coded = jnp.where(column == width + j, scale, coded)
    out[:, here.start :] = coded.astype(jnp.bfloat16)


def decode(ref, j, here, width, rows=slice(None)):
    coded = ref[rows, here].astype(jnp.float32)
    scale = ref[rows, width + j : width + j + 1].astype(jnp.float32) * (1.0 / REACH)
    size = jnp.abs(coded)
    root = jnp.where(size > 0.0, jnp.exp(jnp.log(size) * (1.0 / POWER)), 0.0)
    return jnp.where(coded < 0.0, -root, root) * scale


def split3(value):
    high = value.astype(jnp.bfloat16)
    rest = value - high.astype(jnp.float32)
    middle = rest.astype(jnp.bfloat16)
    low = (rest - middle.astype(jnp.float32)).astype(jnp.bfloat16)
    return high, middle, low


def pieces3(value):
    high = lax.reduce_precision(value, 8, 7)
    middle = lax.reduce_precision(value - high, 8, 7)
    return [p.astype(jnp.bfloat16) for p in (high, middle, value - high - middle)]


def dot(left, right):
    return jnp.dot(left, right, preferred_element_type=jnp.float32)


def dot_t(left, right):
    return lax.dot_general(
        left, right, (((1,), (1,)), ((), ())), preferred_element_type=jnp.float32
    )


def partial_kernel(width, layout, n, base, *refs):
    pieces, (wo, wr, uo, ur, down, own, *outs, held, low, kept_scales, sems) = refs[:n], refs[n:]
    j = pl.program_id(0)
    rows = own.shape[0]
    half = wo.shape[1]
    full = width // TILE
    rest = width - full * TILE
    tail = own.shape[1] // 128 * 128
    column = lax.broadcasted_iota(jnp.int32, (rows, 128), 1)

    @pl.when(j == 0)
    def _():
        gathers = []
        for i, (which, start, size, step, offset) in enumerate(layout):
            at = pl.multiple_of(lax.rem(base[0] + step, 4) * rows + offset, 16)
            gathers.append(pltpu.make_async_copy(pieces[which].at[pl.ds(start, size)], held.at[pl.ds(at, size)], sems.at[i]))
            gathers[-1].start()
        for copy in gathers:
            copy.wait()
        total = dot_t(held[:, :half], uo[...]) + dot_t(held[:, half:], ur[...])
        low[...] = jnp.concatenate(split3(total), axis=1)
        kept_scales[...] = jnp.zeros_like(kept_scales)

    def sums(size):
        value = dot_t(held[:, :half], wo[:size, :]) + dot_t(held[:, half:], wr[:size, :]) + dot(low[...], down[:, :size])
        for d in range(3):
            coded, scale = encode(value[(d + 1) * rows : (d + 2) * rows])
            kept_scales[d] = jnp.where(column == width % 128 + j, scale, kept_scales[d])
            yield value, d, coded

    @pl.when(j < full)
    def _():
        here = pl.ds(pl.multiple_of(j * TILE, TILE), TILE)
        for value, d, coded in sums(TILE):
            outs[d][:, here] = coded.astype(jnp.bfloat16)
        own[:, here] = value[:rows]

    @pl.when(j == full)
    def _():
        for value, d, coded in sums(rest):
            before = tail - full * TILE
            outs[d][:, full * TILE : tail] = coded[:, :before].astype(jnp.bfloat16)
            last = jnp.concatenate([coded[:, before:], jnp.zeros((rows, 128 - (width - tail)), jnp.float32)], axis=1)
            outs[d][:, tail:] = jnp.where(column < width - tail, last, kept_scales[d]).astype(jnp.bfloat16)
        own[:, full * TILE :] = value[:rows]


def partial(base, pieces, layout, wo, wr, uo, ur, down):
    width, half = wo.shape
    rows = sum(size for _, _, size, _, _ in layout) // 4
    padded = (width // 128 + 1) * 128
    hbm = pl.BlockSpec(memory_space=pltpu.HBM)
    strip = lambda a: pl.BlockSpec((TILE, a.shape[1]), lambda j, b: (j, 0))
    whole = lambda a: pl.BlockSpec(a.shape, lambda j, b: (0, 0))
    return pl.pallas_call(
        functools.partial(partial_kernel, width, layout, len(pieces)),
        grid_spec=pltpu.PrefetchScalarGridSpec(
            num_scalar_prefetch=1,
            grid=(width // TILE + 1,),
            in_specs=[hbm] * len(pieces) + [
                strip(wo),
                strip(wr),
                whole(uo),
                whole(ur),
                pl.BlockSpec((down.shape[0], TILE), lambda j, b: (0, j)),
            ],
            out_specs=[pl.BlockSpec((rows, width), lambda j, b: (0, 0))]
            + [pl.BlockSpec((rows, padded), lambda j, b: (0, 0))] * 3,
            scratch_shapes=[
                pltpu.VMEM((4 * rows, 2 * half), jnp.bfloat16),
                pltpu.VMEM((4 * rows, 48), jnp.bfloat16),
                pltpu.VMEM((3, rows, 128), jnp.float32),
                pltpu.SemaphoreType.DMA((len(layout),)),
            ],
        ),
        out_shape=[jax.ShapeDtypeStruct((rows, width), jnp.float32)]
        + [jax.ShapeDtypeStruct((rows, padded), jnp.bfloat16)] * 3,
        compiler_params=pltpu.CompilerParams(vmem_limit_bytes=KERNEL_BYTES),
        cost_estimate=pl.CostEstimate(flops=PRETEND, bytes_accessed=1, transcendentals=0),
        name="partial",
    )(base, *pieces, wo, wr, uo, ur, down)


def half_kernel(which, width, layout, n, base, *refs):
    pieces, (wo, wr, uo, ur, down, own, *outs, held, held_wo, held_wr, low, total, sems, w_sems) = refs[:n], refs[n:]
    rows = own.shape[0]
    half = wo.shape[1]
    always = base[0] >= 0
    strip = pl.ds(which * width, width)
    first = pltpu.make_async_copy(wo.at[strip], held_wo, w_sems.at[0])
    second = pltpu.make_async_copy(wr.at[strip], held_wr, w_sems.at[1])
    gathers = []
    for i, (piece, start, size, step, offset) in enumerate(layout):
        at = pl.multiple_of(lax.rem(base[0] + step, 4) * rows + offset, 16)
        gathers.append(pltpu.make_async_copy(pieces[piece].at[pl.ds(start, size)], held.at[pl.ds(at, size)], sems.at[i]))
        gathers[-1].start()
    first.start()
    second.start()

    @pl.when(always)
    def _():
        for copy in gathers:
            copy.wait()
        factors = dot_t(held[:, :half], uo[...]) + dot_t(held[:, half:], ur[...])
        low[...] = jnp.concatenate(split3(factors), axis=1)

    @pl.when(always)
    def _():
        first.wait()
        for _, here in tiles(width):
            shift = slice(which * width + here.start, which * width + here.stop)
            total[:, here] = dot_t(held[:, :half], held_wo[here, :]) + dot(low[...], down[:, shift])

    @pl.when(always)
    def _():
        second.wait()
        scales = [[], [], []]
        for j, here in tiles(width):
            value = total[:, here] + dot_t(held[:, half:], held_wr[here, :])
            own[:, here] = value[:rows]
            for d, out in enumerate(outs):
                coded, scale = encode(value[(d + 1) * rows : (d + 2) * rows])
                scales[d].append(scale)
                put(out, here, coded, scales[d], width)


def partial_half(which, base, pieces, layout, wo, wr, uo, ur, down):
    width, half = wo.shape[0] // 2, wo.shape[1]
    rows = sum(size for _, _, size, _, _ in layout) // 4
    padded = (width // 128 + 1) * 128
    hbm = pl.BlockSpec(memory_space=pltpu.HBM)
    whole = lambda a: pl.BlockSpec(a.shape, lambda j, b: (0, 0))
    return pl.pallas_call(
        functools.partial(half_kernel, which, width, layout, len(pieces)),
        grid_spec=pltpu.PrefetchScalarGridSpec(
            num_scalar_prefetch=1,
            grid=(1,),
            in_specs=[hbm] * (len(pieces) + 2) + [whole(uo), whole(ur), whole(down)],
            out_specs=[pl.BlockSpec((rows, width), lambda j, b: (0, 0))]
            + [pl.BlockSpec((rows, padded), lambda j, b: (0, 0))] * 3,
            scratch_shapes=[
                pltpu.VMEM((4 * rows, 2 * half), jnp.bfloat16),
                pltpu.VMEM((width, half), jnp.bfloat16),
                pltpu.VMEM((width, half), jnp.bfloat16),
                pltpu.VMEM((4 * rows, 48), jnp.bfloat16),
                pltpu.VMEM((4 * rows, width), jnp.float32),
                pltpu.SemaphoreType.DMA((len(layout),)),
                pltpu.SemaphoreType.DMA((2,)),
            ],
        ),
        out_shape=[jax.ShapeDtypeStruct((rows, width), jnp.float32)]
        + [jax.ShapeDtypeStruct((rows, padded), jnp.bfloat16)] * 3,
        compiler_params=pltpu.CompilerParams(vmem_limit_bytes=KERNEL_BYTES),
        cost_estimate=pl.CostEstimate(flops=PRETEND, bytes_accessed=1, transcendentals=0),
        name="partial_half",
    )(base, *pieces, wo, wr, uo, ur, down)


def fold_kernel(width, swap, own, a, b, c, keep, send):
    rows = keep.shape[0]
    swapped = swap[0] == 1
    scales = []
    for j, here in tiles(width):
        total = own[:, here]
        for r in (a, b, c):
            total = total + decode(r, j, here, width)
        first, second = total[:rows], total[rows:]
        keep[:, here] = jnp.where(swapped, second, first)
        coded, scale = encode(jnp.where(swapped, first, second))
        scales.append(scale)
        put(send, here, coded, scales, width)


def fold(swap, own, received, width):
    rows = own.shape[0]
    padded = received[0].shape[1]
    vmem = pl.BlockSpec(memory_space=pltpu.VMEM)
    return pl.pallas_call(
        functools.partial(fold_kernel, width),
        in_specs=[pl.BlockSpec(memory_space=pltpu.SMEM)] + [vmem] * 4,
        out_specs=[vmem] * 2,
        out_shape=[
            jax.ShapeDtypeStruct((rows // 2, width), jnp.float32),
            jax.ShapeDtypeStruct((rows // 2, padded), jnp.bfloat16),
        ],
        cost_estimate=pl.CostEstimate(flops=1, bytes_accessed=1, transcendentals=0),
        name="fold",
    )(swap, own, *received)


def finish_kernel(keep0, got0, keep1, got1, keep2, got2, out, total):
    rows, width = keep0.shape
    for j, here in tiles(width):
        total[:rows, here] = keep0[:, here] + decode(got0, j, here, width)
    halves = []
    for keep, got in ((keep1, got1), (keep2, got2)):
        for j, here in tiles(keep.shape[1]):
            halves.append(keep[:, here] + decode(got, j, here, keep.shape[1]))
    total[rows:, :] = jnp.concatenate(halves, axis=1)
    for at in range(0, width, 256):
        here = slice(at, min(at + 256, width))
        out[here, :] = total[:, here].T.astype(out.dtype)


def finish(*keeps_and_gots):
    vmem = pl.BlockSpec(memory_space=pltpu.VMEM)
    keep0, _, keep1 = keeps_and_gots[:3]
    shape = (keep0.shape[0] + keep1.shape[0], keep0.shape[1])
    return pl.pallas_call(
        finish_kernel,
        in_specs=[vmem] * 6,
        out_specs=vmem,
        out_shape=jax.ShapeDtypeStruct(shape[::-1], jnp.bfloat16),
        scratch_shapes=[pltpu.VMEM(shape, jnp.float32)],
        name="finish",
    )(*keeps_and_gots)


def ahead(array, axis, step):
    n = SIZES[AXES.index(axis)]
    return lax.ppermute(array, axis, [(i, (i + step) % n) for i in range(n)])


def across(array, axis, bit):
    n = SIZES[AXES.index(axis)]
    return lax.ppermute(array, axis, [(i, i ^ bit) for i in range(n)])


def after(array, *others):
    return lax.optimization_barrier((array, *others))[0]


def phase(*arrays):
    return lax.optimization_barrier(arrays)


PARTS = (64, 64)


def on_device(inputs, cotangent, weight, adapter_down_factor, adapter_up_factor):
    y, xl, core, z, xh = (lax.axis_index(a) for a in AXES)
    row_position = (y * 2 + xl) * 2 + core
    column_position = z * 2 + xh
    tokens, hidden = cotangent.shape
    width_row_block = inputs.shape[1]
    width = weight.shape[0]
    rows = tokens // 2
    p = rows * PARTS[0] // sum(PARTS)
    q = rows - p
    h = p // 2
    base = jnp.reshape(lax.rem(z - y + 4, 4), (1,)).astype(jnp.int32)
    swap = jnp.reshape(xl ^ xh, (1,)).astype(jnp.int32)

    mine = lax.dynamic_slice_in_dim(cotangent, core * rows, rows, 0)
    theirs = lax.dynamic_slice_in_dim(cotangent, (1 - core) * rows, rows, 0)
    other = across(theirs, "core", 1)
    block = jnp.concatenate([mine, other], axis=1)

    up_own = lax.dynamic_slice_in_dim(adapter_up_factor, row_position * hidden, hidden, 1)
    up_other = lax.dynamic_slice_in_dim(adapter_up_factor, (row_position ^ 1) * hidden, hidden, 1)
    down_columns = scaling * lax.dynamic_slice_in_dim(adapter_down_factor.T, column_position * width, width, 1)
    down3 = jnp.concatenate([down_columns] * 3, axis=0)
    down_rows = lax.dynamic_slice_in_dim(adapter_down_factor, row_position * width_row_block, width_row_block, 0)

    low_part = dot_t(up_own, after(cotangent, other))
    proj_part = lax.dot_general(down_rows, inputs, (((0,), (1,)), ((), ())), preferred_element_type=jnp.float32)
    rank = low_part.shape[0]
    small = jnp.concatenate([low_part, proj_part], axis=0)

    up1, down1 = ahead(block[:p], "z", 1), ahead(block[:p], "z", 3)
    x0 = across(block[:p], "xh", 1)
    small_other = across(small, "core", 1)
    block, weight, up1, down1, x0, small, small_other = phase(block, weight, up1, down1, x0, small, small_other)
    small = small + small_other

    up2 = ahead(jnp.concatenate([up1[:h], x0], axis=0), "z", 1)
    down2 = ahead(jnp.concatenate([down1[h:], x0], axis=0), "z", 3)
    x1 = across(block[p:], "xh", 1)
    weight_other = across(weight, "core", 1)
    small_other = across(small, "xl", 1)
    block, up2, down2, x1, weight_other, small_other, up_other, down3 = phase(
        block, up2, down2, x1, weight_other, small_other, up_other, down3
    )
    small = small + small_other

    up3, down3z = ahead(up2[h : 2 * h], "z", 1), ahead(down2[2 * h :], "z", 3)
    small_other = across(small, "y", 1)
    pair1 = jnp.concatenate([block[p:], x1], axis=0)
    pair1, up3, down3z, small_other = phase(pair1, up3, down3z, small_other)
    small = small + small_other

    up4, down4 = ahead(pair1, "z", 1), ahead(pair1, "z", 3)
    layout0 = [
        (0, 0, p, 0, 0),
        (1, 0, p, 0, p),
        (2, 0, p, 3, 0),
        (3, 0, p, 1, 0),
        (4, h, p, 3, p),
        (5, h, p, 1, p),
        (4, 0, h, 2, 0),
        (5, 0, h, 2, h),
        (6, 0, h, 2, p),
        (7, 0, h, 2, p + h),
    ]
    kept0, a0, b0, c0 = partial(
        base, (block, x0, up1, down1, up2, down2, up3, down3z), layout0, weight, weight_other, up_own, up_other, down3
    )
    small_other = across(small, "y", 2)
    up4, down4, kept0, a0, b0, c0, small_other = phase(up4, down4, kept0, a0, b0, c0, small_other)
    small = small + small_other

    up5, down5 = ahead(up4[:q], "z", 1), ahead(down4[q:], "z", 3)
    a0, c0 = ahead(a0, "y", 1), ahead(c0, "y", 3)
    low48 = jnp.concatenate(pieces3(scaling * small[:rank]), axis=0)
    proj48 = jnp.concatenate(pieces3(scaling * small[rank:]), axis=0)

    def three(left, right):
        out = jnp.dot(left, right, preferred_element_type=jnp.float32)
        return out[:rank] + (out[rank : 2 * rank] + out[2 * rank :])

    parts = jnp.concatenate([three(low48, inputs), three(proj48, cotangent)], axis=1)
    parts_other = across(parts, "xh", 1)
    up5, down5, a0, c0, b0, parts, parts_other = phase(up5, down5, a0, c0, b0, parts, parts_other)
    parts = parts + parts_other

    layout1 = [
        (0, p, q, 0, 0),
        (1, 0, q, 0, q),
        (2, 0, 2 * q, 3, 0),
        (3, 0, 2 * q, 1, 0),
        (4, 0, q, 2, 0),
        (5, 0, q, 2, q),
    ]

    def half_of_sums(which):
        return partial_half(
            which, base, (block, x1, up4, down4, up5, down5), layout1, weight, weight_other, up_own, up_other, down3
        )

    b0 = ahead(b0, "y", 2)
    kept1, a1, b1, c1 = half_of_sums(0)
    kept1, a1, b1, c1, b0, parts, block = phase(kept1, a1, b1, c1, b0, parts, block)

    a1, c1, b1 = ahead(a1, "y", 1), ahead(c1, "y", 3), ahead(b1, "y", 2)
    parts_other = across(parts, "z", 1)
    kept2, a2, b2, c2 = half_of_sums(1)
    kept2, a2, b2, c2, a1, c1, b1, b0, parts_other = phase(kept2, a2, b2, c2, a1, c1, b1, b0, parts_other)
    parts = parts + parts_other

    a2, c2, b2 = ahead(a2, "y", 1), ahead(c2, "y", 3), ahead(b2, "y", 2)
    parts_other = across(parts, "z", 2)
    keep0, send0 = fold(swap, kept0, (a0, c0, b0), width)
    keep1, send1 = fold(swap, kept1, (a1, c1, b1), width // 2)
    a2, c2, b2, keep0, send0, keep1, send1, parts_other = phase(a2, c2, b2, keep0, send0, keep1, send1, parts_other)

    got0, got1 = across(send0, "xl", 1), across(send1, "xl", 1)
    keep2, send2 = fold(swap, kept2, (a2, c2, b2), width // 2)
    got2 = across(send2, "xl", 1)
    parts = after(parts, send2) + parts_other
    grad_a = parts[:, :width_row_block].T
    grad_b = parts[:, width_row_block:]
    got0, got1, got2, grad_a, grad_b = phase(got0, got1, got2, grad_a, grad_b)
    grad_input = finish(keep0, got0, keep1, got1, keep2, got2).T
    return grad_input, grad_a, grad_b


def solution(mesh):
    fine = Mesh(mesh.devices.reshape(SIZES), AXES)
    in_specs = (P(COL, ROW), P(COL, ROW), P(COL, ROW), P(), P())
    out_specs = (P(ROW, COL), P(ROW, None), P(None, ROW))
    return jax.shard_map(on_device, mesh=fine, in_specs=in_specs, out_specs=out_specs, check_vma=False)
```

```python
import functools

import jax
import jax.numpy as jnp
from jax import lax
from jax.experimental import pallas as pl
from jax.experimental.pallas import tpu as pltpu
from jax.sharding import Mesh, PartitionSpec as P

scaling = 2.0
AXES = ("y", "xl", "core", "z", "xh")
SIZES = (4, 2, 2, 4, 2)
ROW = ("y", "xl", "core")
COL = ("z", "xh")

POWER = 17
REACH = 170.0
SMALLEST = 1e-35
TILE = 512
KERNEL_BYTES = 58 << 20
PRETEND = 1


def tiles(width):
    return [(j, slice(at, min(at + TILE, width))) for j, at in enumerate(range(0, width, TILE))]


def encode(value):
    largest = jnp.max(jnp.abs(value), axis=1, keepdims=True)
    scale = jnp.maximum(largest * 1.01, SMALLEST).astype(jnp.bfloat16).astype(jnp.float32)
    a = value * (REACH / scale)
    a2 = a * a
    a4 = a2 * a2
    a8 = a4 * a4
    return a8 * a8 * a, scale


def put(out, here, coded, scales, width):
    if here.stop < width:
        out[:, here] = coded.astype(jnp.bfloat16)
        return
    coded = jnp.concatenate([coded, jnp.zeros((coded.shape[0], out.shape[1] - width), jnp.float32)], axis=1)
    column = lax.broadcasted_iota(jnp.int32, coded.shape, 1) + here.start
    for j, scale in enumerate(scales):
        coded = jnp.where(column == width + j, scale, coded)
    out[:, here.start :] = coded.astype(jnp.bfloat16)


def decode(ref, j, here, width, rows=slice(None)):
    coded = ref[rows, here].astype(jnp.float32)
    scale = ref[rows, width + j : width + j + 1].astype(jnp.float32) * (1.0 / REACH)
    size = jnp.abs(coded)
    root = jnp.where(size > 0.0, jnp.exp(jnp.log(size) * (1.0 / POWER)), 0.0)
    return jnp.where(coded < 0.0, -root, root) * scale


def split3(value):
    high = value.astype(jnp.bfloat16)
    rest = value - high.astype(jnp.float32)
    middle = rest.astype(jnp.bfloat16)
    low = (rest - middle.astype(jnp.float32)).astype(jnp.bfloat16)
    return high, middle, low


def pieces3(value):
    high = lax.reduce_precision(value, 8, 7)
    middle = lax.reduce_precision(value - high, 8, 7)
    return [p.astype(jnp.bfloat16) for p in (high, middle, value - high - middle)]


def dot(left, right):
    return jnp.dot(left, right, preferred_element_type=jnp.float32)


def dot_t(left, right):
    return lax.dot_general(
        left, right, (((1,), (1,)), ((), ())), preferred_element_type=jnp.float32
    )


def partial_kernel(width, layout, n, base, *refs):
    pieces, (wo, wr, uo, ur, down, own, *outs, held, low, kept_scales, sems) = refs[:n], refs[n:]
    j = pl.program_id(0)
    rows = own.shape[0]
    half = wo.shape[1]
    full = width // TILE
    rest = width - full * TILE
    tail = own.shape[1] // 128 * 128
    column = lax.broadcasted_iota(jnp.int32, (rows, 128), 1)

    @pl.when(j == 0)
    def _():
        gathers = []
        for i, (which, start, size, step, offset) in enumerate(layout):
            at = pl.multiple_of(lax.rem(base[0] + step, 4) * rows + offset, 16)
            gathers.append(pltpu.make_async_copy(pieces[which].at[pl.ds(start, size)], held.at[pl.ds(at, size)], sems.at[i]))
            gathers[-1].start()
        for copy in gathers:
            copy.wait()
        total = dot_t(held[:, :half], uo[...]) + dot_t(held[:, half:], ur[...])
        low[...] = jnp.concatenate(split3(total), axis=1)
        kept_scales[...] = jnp.zeros_like(kept_scales)

    def sums(size):
        value = dot_t(held[:, :half], wo[:size, :]) + dot_t(held[:, half:], wr[:size, :]) + dot(low[...], down[:, :size])
        for d in range(3):
            coded, scale = encode(value[(d + 1) * rows : (d + 2) * rows])
            kept_scales[d] = jnp.where(column == width % 128 + j, scale, kept_scales[d])
            yield value, d, coded

    @pl.when(j < full)
    def _():
        here = pl.ds(pl.multiple_of(j * TILE, TILE), TILE)
        for value, d, coded in sums(TILE):
            outs[d][:, here] = coded.astype(jnp.bfloat16)
        own[:, here] = value[:rows]

    @pl.when(j == full)
    def _():
        for value, d, coded in sums(rest):
            before = tail - full * TILE
            outs[d][:, full * TILE : tail] = coded[:, :before].astype(jnp.bfloat16)
            last = jnp.concatenate([coded[:, before:], jnp.zeros((rows, 128 - (width - tail)), jnp.float32)], axis=1)
            outs[d][:, tail:] = jnp.where(column < width - tail, last, kept_scales[d]).astype(jnp.bfloat16)
        own[:, full * TILE :] = value[:rows]


def partial(base, pieces, layout, wo, wr, uo, ur, down):
    width, half = wo.shape
    rows = sum(size for _, _, size, _, _ in layout) // 4
    padded = (width // 128 + 1) * 128
    hbm = pl.BlockSpec(memory_space=pltpu.HBM)
    strip = lambda a: pl.BlockSpec((TILE, a.shape[1]), lambda j, b: (j, 0))
    whole = lambda a: pl.BlockSpec(a.shape, lambda j, b: (0, 0))
    return pl.pallas_call(
        functools.partial(partial_kernel, width, layout, len(pieces)),
        grid_spec=pltpu.PrefetchScalarGridSpec(
            num_scalar_prefetch=1,
            grid=(width // TILE + 1,),
            in_specs=[hbm] * len(pieces) + [
                strip(wo),
                strip(wr),
                whole(uo),
                whole(ur),
                pl.BlockSpec((down.shape[0], TILE), lambda j, b: (0, j)),
            ],
            out_specs=[pl.BlockSpec((rows, width), lambda j, b: (0, 0))]
            + [pl.BlockSpec((rows, padded), lambda j, b: (0, 0))] * 3,
            scratch_shapes=[
                pltpu.VMEM((4 * rows, 2 * half), jnp.bfloat16),
                pltpu.VMEM((4 * rows, 48), jnp.bfloat16),
                pltpu.VMEM((3, rows, 128), jnp.float32),
                pltpu.SemaphoreType.DMA((len(layout),)),
            ],
        ),
        out_shape=[jax.ShapeDtypeStruct((rows, width), jnp.float32)]
        + [jax.ShapeDtypeStruct((rows, padded), jnp.bfloat16)] * 3,
        compiler_params=pltpu.CompilerParams(vmem_limit_bytes=KERNEL_BYTES),
        cost_estimate=pl.CostEstimate(flops=PRETEND, bytes_accessed=1, transcendentals=0),
        name="partial",
    )(base, *pieces, wo, wr, uo, ur, down)


def half_kernel(which, width, layout, n, base, *refs):
    pieces, (wo, wr, uo, ur, down, own, *outs, held, held_wo, held_wr, low, total, sems, w_sems) = refs[:n], refs[n:]
    rows = own.shape[0]
    half = wo.shape[1]
    always = base[0] >= 0
    strip = pl.ds(which * width, width)
    first = pltpu.make_async_copy(wo.at[strip], held_wo, w_sems.at[0])
    second = pltpu.make_async_copy(wr.at[strip], held_wr, w_sems.at[1])
    gathers = []
    for i, (piece, start, size, step, offset) in enumerate(layout):
        at = pl.multiple_of(lax.rem(base[0] + step, 4) * rows + offset, 16)
        gathers.append(pltpu.make_async_copy(pieces[piece].at[pl.ds(start, size)], held.at[pl.ds(at, size)], sems.at[i]))
        gathers[-1].start()
    first.start()
    second.start()

    @pl.when(always)
    def _():
        for copy in gathers:
            copy.wait()
        factors = dot_t(held[:, :half], uo[...]) + dot_t(held[:, half:], ur[...])
        low[...] = jnp.concatenate(split3(factors), axis=1)

    @pl.when(always)
    def _():
        first.wait()
        for _, here in tiles(width):
            shift = slice(which * width + here.start, which * width + here.stop)
            total[:, here] = dot_t(held[:, :half], held_wo[here, :]) + dot(low[...], down[:, shift])

    @pl.when(always)
    def _():
        second.wait()
        scales = [[], [], []]
        for j, here in tiles(width):
            value = total[:, here] + dot_t(held[:, half:], held_wr[here, :])
            own[:, here] = value[:rows]
            for d, out in enumerate(outs):
                coded, scale = encode(value[(d + 1) * rows : (d + 2) * rows])
                scales[d].append(scale)
                put(out, here, coded, scales[d], width)


def partial_half(which, base, pieces, layout, wo, wr, uo, ur, down):
    width, half = wo.shape[0] // 2, wo.shape[1]
    rows = sum(size for _, _, size, _, _ in layout) // 4
    padded = (width // 128 + 1) * 128
    hbm = pl.BlockSpec(memory_space=pltpu.HBM)
    whole = lambda a: pl.BlockSpec(a.shape, lambda j, b: (0, 0))
    return pl.pallas_call(
        functools.partial(half_kernel, which, width, layout, len(pieces)),
        grid_spec=pltpu.PrefetchScalarGridSpec(
            num_scalar_prefetch=1,
            grid=(1,),
            in_specs=[hbm] * (len(pieces) + 2) + [whole(uo), whole(ur), whole(down)],
            out_specs=[pl.BlockSpec((rows, width), lambda j, b: (0, 0))]
            + [pl.BlockSpec((rows, padded), lambda j, b: (0, 0))] * 3,
            scratch_shapes=[
                pltpu.VMEM((4 * rows, 2 * half), jnp.bfloat16),
                pltpu.VMEM((width, half), jnp.bfloat16),
                pltpu.VMEM((width, half), jnp.bfloat16),
                pltpu.VMEM((4 * rows, 48), jnp.bfloat16),
                pltpu.VMEM((4 * rows, width), jnp.float32),
                pltpu.SemaphoreType.DMA((len(layout),)),
                pltpu.SemaphoreType.DMA((2,)),
            ],
        ),
        out_shape=[jax.ShapeDtypeStruct((rows, width), jnp.float32)]
        + [jax.ShapeDtypeStruct((rows, padded), jnp.bfloat16)] * 3,
        compiler_params=pltpu.CompilerParams(vmem_limit_bytes=KERNEL_BYTES),
        cost_estimate=pl.CostEstimate(flops=PRETEND, bytes_accessed=1, transcendentals=0),
        name="partial_half",
    )(base, *pieces, wo, wr, uo, ur, down)


def fold_kernel(width, swap, own, a, b, c, keep, send):
    rows = keep.shape[0]
    swapped = swap[0] == 1
    scales = []
    for j, here in tiles(width):
        total = own[:, here]
        for r in (a, b, c):
            total = total + decode(r, j, here, width)
        first, second = total[:rows], total[rows:]
        keep[:, here] = jnp.where(swapped, second, first)
        coded, scale = encode(jnp.where(swapped, first, second))
        scales.append(scale)
        put(send, here, coded, scales, width)


def fold(swap, own, received, width):
    rows = own.shape[0]
    padded = received[0].shape[1]
    vmem = pl.BlockSpec(memory_space=pltpu.VMEM)
    return pl.pallas_call(
        functools.partial(fold_kernel, width),
        in_specs=[pl.BlockSpec(memory_space=pltpu.SMEM)] + [vmem] * 4,
        out_specs=[vmem] * 2,
        out_shape=[
            jax.ShapeDtypeStruct((rows // 2, width), jnp.float32),
            jax.ShapeDtypeStruct((rows // 2, padded), jnp.bfloat16),
        ],
        cost_estimate=pl.CostEstimate(flops=1, bytes_accessed=1, transcendentals=0),
        name="fold",
    )(swap, own, *received)


def finish_kernel(keep0, got0, keep1, got1, keep2, got2, out, total):
    rows, width = keep0.shape
    for j, here in tiles(width):
        total[:rows, here] = keep0[:, here] + decode(got0, j, here, width)
    halves = []
    for keep, got in ((keep1, got1), (keep2, got2)):
        for j, here in tiles(keep.shape[1]):
            halves.append(keep[:, here] + decode(got, j, here, keep.shape[1]))
    total[rows:, :] = jnp.concatenate(halves, axis=1)
    for at in range(0, width, 256):
        here = slice(at, min(at + 256, width))
        out[here, :] = total[:, here].T.astype(out.dtype)


def finish(*keeps_and_gots):
    vmem = pl.BlockSpec(memory_space=pltpu.VMEM)
    keep0, _, keep1 = keeps_and_gots[:3]
    shape = (keep0.shape[0] + keep1.shape[0], keep0.shape[1])
    return pl.pallas_call(
        finish_kernel,
        in_specs=[vmem] * 6,
        out_specs=vmem,
        out_shape=jax.ShapeDtypeStruct(shape[::-1], jnp.bfloat16),
        scratch_shapes=[pltpu.VMEM(shape, jnp.float32)],
        name="finish",
    )(*keeps_and_gots)


def ahead(array, axis, step):
    n = SIZES[AXES.index(axis)]
    return lax.ppermute(array, axis, [(i, (i + step) % n) for i in range(n)])


def across(array, axis, bit):
    n = SIZES[AXES.index(axis)]
    return lax.ppermute(array, axis, [(i, i ^ bit) for i in range(n)])


def after(array, *others):
    return lax.optimization_barrier((array, *others))[0]


def phase(*arrays):
    return lax.optimization_barrier(arrays)


PARTS = (64, 64)


def on_device(inputs, cotangent, weight, adapter_down_factor, adapter_up_factor):
    y, xl, core, z, xh = (lax.axis_index(a) for a in AXES)
    row_position = (y * 2 + xl) * 2 + core
    column_position = z * 2 + xh
    tokens, hidden = cotangent.shape
    width_row_block = inputs.shape[1]
    width = weight.shape[0]
    rows = tokens // 2
    p = rows * PARTS[0] // sum(PARTS)
    q = rows - p
    base = jnp.reshape(lax.rem(z - y + 4, 4), (1,)).astype(jnp.int32)
    swap = jnp.reshape(xl ^ xh, (1,)).astype(jnp.int32)

    mine = lax.dynamic_slice_in_dim(cotangent, core * rows, rows, 0)
    theirs = lax.dynamic_slice_in_dim(cotangent, (1 - core) * rows, rows, 0)
    other = across(theirs, "core", 1)
    block = jnp.concatenate([mine, other], axis=1)

    up_own = lax.dynamic_slice_in_dim(adapter_up_factor, row_position * hidden, hidden, 1)
    up_other = lax.dynamic_slice_in_dim(adapter_up_factor, (row_position ^ 1) * hidden, hidden, 1)
    down_columns = scaling * lax.dynamic_slice_in_dim(adapter_down_factor.T, column_position * width, width, 1)
    down3 = jnp.concatenate([down_columns] * 3, axis=0)
    down_rows = lax.dynamic_slice_in_dim(adapter_down_factor, row_position * width_row_block, width_row_block, 0)

    low_part = dot_t(up_own, after(cotangent, other))
    proj_part = lax.dot_general(down_rows, inputs, (((0,), (1,)), ((), ())), preferred_element_type=jnp.float32)
    rank = low_part.shape[0]
    small = jnp.concatenate([low_part, proj_part], axis=0)

    up1, down1 = ahead(block[:p], "z", 1), ahead(block[:p], "z", 3)
    far1 = ahead(block[:p], "z", 2)
    x0, x1 = across(block[:p], "xh", 1), across(block[p:], "xh", 1)
    block, weight, up1, down1, far1, x0, x1, small = phase(block, weight, up1, down1, far1, x0, x1, small)

    up2, down2 = ahead(x0, "z", 1), ahead(x0, "z", 3)
    far2 = across(far1, "xh", 1)
    weight_other = across(weight, "core", 1)
    pair1 = jnp.concatenate([block[p:], x1], axis=0)
    small = small + across(small, "core", 1)
    small = small + across(small, "y", 1)
    small_other = across(small, "y", 2)
    block, up2, down2, far2, weight_other, pair1, small, small_other, up_other, down3 = phase(
        block, up2, down2, far2, weight_other, pair1, small, small_other, up_other, down3
    )
    small = small + small_other

    up4, down4 = ahead(pair1, "z", 1), ahead(pair1, "z", 3)
    layout0 = [(i, 0, p, step, i % 2 * p) for i, step in enumerate((0, 0, 3, 3, 1, 1, 2, 2))]
    kept0, a0, b0, c0 = partial(
        base, (block, x0, up1, up2, down1, down2, far1, far2), layout0, weight, weight_other, up_own, up_other, down3
    )
    small_other = across(small, "xl", 1)
    up4, down4, kept0, a0, b0, c0, small, small_other = phase(up4, down4, kept0, a0, b0, c0, small, small_other)
    small = small + small_other

    up5, down5 = ahead(up4[:q], "z", 1), ahead(down4[q:], "z", 3)
    a0, c0 = ahead(a0, "y", 1), ahead(c0, "y", 3)
    low48 = jnp.concatenate(pieces3(scaling * small[:rank]), axis=0)
    proj48 = jnp.concatenate(pieces3(scaling * small[rank:]), axis=0)

    def three(left, right):
        out = jnp.dot(left, right, preferred_element_type=jnp.float32)
        return out[:rank] + (out[rank : 2 * rank] + out[2 * rank :])

    parts = jnp.concatenate([three(low48, inputs), three(proj48, cotangent)], axis=1)
    parts_other = across(parts, "xh", 1)
    up5, down5, a0, c0, b0, parts, parts_other = phase(up5, down5, a0, c0, b0, parts, parts_other)
    parts = parts + parts_other

    layout1 = [
        (0, p, q, 0, 0),
        (1, 0, q, 0, q),
        (2, 0, 2 * q, 3, 0),
        (3, 0, 2 * q, 1, 0),
        (4, 0, q, 2, 0),
        (5, 0, q, 2, q),
    ]

    def half_of_sums(which):
        return partial_half(
            which, base, (block, x1, up4, down4, up5, down5), layout1, weight, weight_other, up_own, up_other, down3
        )

    b0 = ahead(b0, "y", 2)
    kept1, a1, b1, c1 = half_of_sums(0)
    kept1, a1, b1, c1, b0, parts, block = phase(kept1, a1, b1, c1, b0, parts, block)

    a1, c1, b1 = ahead(a1, "y", 1), ahead(c1, "y", 3), ahead(b1, "y", 2)
    parts_other = across(parts, "z", 1)
    kept2, a2, b2, c2 = half_of_sums(1)
    kept2, a2, b2, c2, a1, c1, b1, b0, parts_other = phase(kept2, a2, b2, c2, a1, c1, b1, b0, parts_other)
    parts = parts + parts_other

    a2, c2, b2 = ahead(a2, "y", 1), ahead(c2, "y", 3), ahead(b2, "y", 2)
    parts_other = across(parts, "z", 2)
    keep0, send0 = fold(swap, kept0, (a0, c0, b0), width)
    keep1, send1 = fold(swap, kept1, (a1, c1, b1), width // 2)
    got1 = across(send1, "xl", 1)
    a2, c2, b2, keep0, send0, keep1, got1, parts_other = phase(a2, c2, b2, keep0, send0, keep1, got1, parts_other)

    got0 = across(send0, "xl", 1)
    keep2, send2 = fold(swap, kept2, (a2, c2, b2), width // 2)
    got2 = across(send2, "xl", 1)
    parts = after(parts, send2) + parts_other
    grad_a = parts[:, :width_row_block].T
    grad_b = parts[:, width_row_block:]
    got0, got2, grad_a, grad_b = phase(got0, got2, grad_a, grad_b)
    grad_input = finish(keep0, got0, keep1, got1, keep2, got2).T
    return grad_input, grad_a, grad_b


def solution(mesh):
    fine = Mesh(mesh.devices.reshape(SIZES), AXES)
    in_specs = (P(COL, ROW), P(COL, ROW), P(COL, ROW), P(), P())
    out_specs = (P(ROW, COL), P(ROW, None), P(None, ROW))
    return jax.shard_map(on_device, mesh=fine, in_specs=in_specs, out_specs=out_specs, check_vma=False)
```

```python
import functools

import jax
import jax.numpy as jnp
from jax import lax
from jax.experimental import pallas as pl
from jax.experimental.pallas import tpu as pltpu
from jax.sharding import Mesh, PartitionSpec as P

scaling = 2.0
AXES = ("y", "xl", "core", "z", "xh")
SIZES = (4, 2, 2, 4, 2)
ROW = ("y", "xl", "core")
COL = ("z", "xh")

POWER = 17
REACH = 170.0
SMALLEST = 1e-35
TILE = 512
KERNEL_BYTES = 58 << 20
PRETEND = 1


def tiles(width):
    return [(j, slice(at, min(at + TILE, width))) for j, at in enumerate(range(0, width, TILE))]


def encode(value):
    largest = jnp.max(jnp.abs(value), axis=1, keepdims=True)
    scale = jnp.maximum(largest * 1.01, SMALLEST).astype(jnp.bfloat16).astype(jnp.float32)
    a = value * (REACH / scale)
    a2 = a * a
    a4 = a2 * a2
    a8 = a4 * a4
    return a8 * a8 * a, scale


def put(out, here, coded, scales, width):
    if here.stop < width:
        out[:, here] = coded.astype(jnp.bfloat16)
        return
    coded = jnp.concatenate([coded, jnp.zeros((coded.shape[0], out.shape[1] - width), jnp.float32)], axis=1)
    column = lax.broadcasted_iota(jnp.int32, coded.shape, 1) + here.start
    for j, scale in enumerate(scales):
        coded = jnp.where(column == width + j, scale, coded)
    out[:, here.start :] = coded.astype(jnp.bfloat16)


def decode(ref, j, here, width, rows=slice(None)):
    coded = ref[rows, here].astype(jnp.float32)
    scale = ref[rows, width + j : width + j + 1].astype(jnp.float32) * (1.0 / REACH)
    size = jnp.abs(coded)
    root = jnp.where(size > 0.0, jnp.exp(jnp.log(size) * (1.0 / POWER)), 0.0)
    return jnp.where(coded < 0.0, -root, root) * scale


def split3(value):
    high = value.astype(jnp.bfloat16)
    rest = value - high.astype(jnp.float32)
    middle = rest.astype(jnp.bfloat16)
    low = (rest - middle.astype(jnp.float32)).astype(jnp.bfloat16)
    return high, middle, low


def pieces3(value):
    high = lax.reduce_precision(value, 8, 7)
    middle = lax.reduce_precision(value - high, 8, 7)
    return [p.astype(jnp.bfloat16) for p in (high, middle, value - high - middle)]


def dot(left, right):
    return jnp.dot(left, right, preferred_element_type=jnp.float32)


def dot_t(left, right):
    return lax.dot_general(
        left, right, (((1,), (1,)), ((), ())), preferred_element_type=jnp.float32
    )


def partial_kernel(width, layout, n, base, *refs):
    pieces, (wo, wr, uo, ur, down, own, *outs, held, low, kept_scales, sems) = refs[:n], refs[n:]
    j = pl.program_id(0)
    rows = own.shape[0]
    half = wo.shape[1]
    full = width // TILE
    rest = width - full * TILE
    tail = own.shape[1] // 128 * 128
    column = lax.broadcasted_iota(jnp.int32, (rows, 128), 1)

    @pl.when(j == 0)
    def _():
        gathers = []
        for i, (which, start, size, step, offset) in enumerate(layout):
            at = pl.multiple_of(lax.rem(base[0] + step, 4) * rows + offset, 16)
            gathers.append(pltpu.make_async_copy(pieces[which].at[pl.ds(start, size)], held.at[pl.ds(at, size)], sems.at[i]))
            gathers[-1].start()
        for copy in gathers:
            copy.wait()
        total = dot_t(held[:, :half], uo[...]) + dot_t(held[:, half:], ur[...])
        low[...] = jnp.concatenate(split3(total), axis=1)
        kept_scales[...] = jnp.zeros_like(kept_scales)

    def sums(size):
        value = dot_t(held[:, :half], wo[:size, :]) + dot_t(held[:, half:], wr[:size, :]) + dot(low[...], down[:, :size])
        for d in range(3):
            coded, scale = encode(value[(d + 1) * rows : (d + 2) * rows])
            kept_scales[d] = jnp.where(column == width % 128 + j, scale, kept_scales[d])
            yield value, d, coded

    @pl.when(j < full)
    def _():
        here = pl.ds(pl.multiple_of(j * TILE, TILE), TILE)
        for value, d, coded in sums(TILE):
            outs[d][:, here] = coded.astype(jnp.bfloat16)
        own[:, here] = value[:rows]

    @pl.when(j == full)
    def _():
        for value, d, coded in sums(rest):
            before = tail - full * TILE
            outs[d][:, full * TILE : tail] = coded[:, :before].astype(jnp.bfloat16)
            last = jnp.concatenate([coded[:, before:], jnp.zeros((rows, 128 - (width - tail)), jnp.float32)], axis=1)
            outs[d][:, tail:] = jnp.where(column < width - tail, last, kept_scales[d]).astype(jnp.bfloat16)
        own[:, full * TILE :] = value[:rows]


def partial(base, pieces, layout, wo, wr, uo, ur, down):
    width, half = wo.shape
    rows = sum(size for _, _, size, _, _ in layout) // 4
    padded = (width // 128 + 1) * 128
    hbm = pl.BlockSpec(memory_space=pltpu.HBM)
    strip = lambda a: pl.BlockSpec((TILE, a.shape[1]), lambda j, b: (j, 0))
    whole = lambda a: pl.BlockSpec(a.shape, lambda j, b: (0, 0))
    return pl.pallas_call(
        functools.partial(partial_kernel, width, layout, len(pieces)),
        grid_spec=pltpu.PrefetchScalarGridSpec(
            num_scalar_prefetch=1,
            grid=(width // TILE + 1,),
            in_specs=[hbm] * len(pieces) + [
                strip(wo),
                strip(wr),
                whole(uo),
                whole(ur),
                pl.BlockSpec((down.shape[0], TILE), lambda j, b: (0, j)),
            ],
            out_specs=[pl.BlockSpec((rows, width), lambda j, b: (0, 0))]
            + [pl.BlockSpec((rows, padded), lambda j, b: (0, 0))] * 3,
            scratch_shapes=[
                pltpu.VMEM((4 * rows, 2 * half), jnp.bfloat16),
                pltpu.VMEM((4 * rows, 48), jnp.bfloat16),
                pltpu.VMEM((3, rows, 128), jnp.float32),
                pltpu.SemaphoreType.DMA((len(layout),)),
            ],
        ),
        out_shape=[jax.ShapeDtypeStruct((rows, width), jnp.float32)]
        + [jax.ShapeDtypeStruct((rows, padded), jnp.bfloat16)] * 3,
        compiler_params=pltpu.CompilerParams(vmem_limit_bytes=KERNEL_BYTES),
        cost_estimate=pl.CostEstimate(flops=PRETEND, bytes_accessed=1, transcendentals=0),
        name="partial",
    )(base, *pieces, wo, wr, uo, ur, down)


def half_kernel(which, width, layout, n, base, *refs):
    pieces, (wo, wr, *given), refs = refs[:n], refs[n:-12], refs[-12:]
    down, own, *outs, low, held, held_wo, held_wr, total, sems, w_sems = refs
    rows = own.shape[0]
    half = wo.shape[1]
    always = base[0] >= 0
    strip = pl.ds(which * width, width)
    first = pltpu.make_async_copy(wo.at[strip], held_wo, w_sems.at[0])
    second = pltpu.make_async_copy(wr.at[strip], held_wr, w_sems.at[1])
    gathers = []
    for i, (piece, start, size, step, offset) in enumerate(layout):
        at = pl.multiple_of(lax.rem(base[0] + step, 4) * rows + offset, 16)
        gathers.append(pltpu.make_async_copy(pieces[piece].at[pl.ds(start, size)], held.at[pl.ds(at, size)], sems.at[i]))
        gathers[-1].start()
    first.start()
    second.start()

    @pl.when(always)
    def _():
        for copy in gathers:
            copy.wait()
        if len(given) == 1:
            low[...] = given[0][...]
        else:
            factors = dot_t(held[:, :half], given[0][...]) + dot_t(held[:, half:], given[1][...])
            low[...] = jnp.concatenate(split3(factors), axis=1)

    @pl.when(always)
    def _():
        first.wait()
        for _, here in tiles(width):
            shift = slice(which * width + here.start, which * width + here.stop)
            total[:, here] = dot_t(held[:, :half], held_wo[here, :]) + dot(low[...], down[:, shift])

    @pl.when(always)
    def _():
        second.wait()
        scales = [[], [], []]
        for j, here in tiles(width):
            value = total[:, here] + dot_t(held[:, half:], held_wr[here, :])
            own[:, here] = value[:rows]
            for d, out in enumerate(outs):
                coded, scale = encode(value[(d + 1) * rows : (d + 2) * rows])
                scales[d].append(scale)
                put(out, here, coded, scales[d], width)


def partial_half(which, base, pieces, layout, wo, wr, given, down):
    width, half = wo.shape[0] // 2, wo.shape[1]
    rows = sum(size for _, _, size, _, _ in layout) // 4
    padded = (width // 128 + 1) * 128
    hbm = pl.BlockSpec(memory_space=pltpu.HBM)
    whole = lambda a: pl.BlockSpec(a.shape, lambda j, b: (0, 0))
    return pl.pallas_call(
        functools.partial(half_kernel, which, width, layout, len(pieces)),
        grid_spec=pltpu.PrefetchScalarGridSpec(
            num_scalar_prefetch=1,
            grid=(1,),
            in_specs=[hbm] * (len(pieces) + 2) + [whole(g) for g in given] + [whole(down)],
            out_specs=[pl.BlockSpec((rows, width), lambda j, b: (0, 0))]
            + [pl.BlockSpec((rows, padded), lambda j, b: (0, 0))] * 3
            + [pl.BlockSpec((4 * rows, 48), lambda j, b: (0, 0))],
            scratch_shapes=[
                pltpu.VMEM((4 * rows, 2 * half), jnp.bfloat16),
                pltpu.VMEM((width, half), jnp.bfloat16),
                pltpu.VMEM((width, half), jnp.bfloat16),
                pltpu.VMEM((4 * rows, width), jnp.float32),
                pltpu.SemaphoreType.DMA((len(layout),)),
                pltpu.SemaphoreType.DMA((2,)),
            ],
        ),
        out_shape=[jax.ShapeDtypeStruct((rows, width), jnp.float32)]
        + [jax.ShapeDtypeStruct((rows, padded), jnp.bfloat16)] * 3
        + [jax.ShapeDtypeStruct((4 * rows, 48), jnp.bfloat16)],
        compiler_params=pltpu.CompilerParams(vmem_limit_bytes=KERNEL_BYTES),
        cost_estimate=pl.CostEstimate(flops=PRETEND, bytes_accessed=1, transcendentals=0),
        name="partial_half",
    )(base, *pieces, wo, wr, *given, down)


def fold_kernel(*refs):
    swapped = refs[0][0] == 1
    n = (len(refs) - 2) // 5
    at = 0
    for i in range(n):
        own, a, b, c = refs[1 + 4 * i : 5 + 4 * i]
        keep, send = refs[1 + 4 * n + i], refs[-1].at[:, pl.ds(at, a.shape[1])]
        at += a.shape[1]
        rows, width = keep.shape
        scales = []
        for j, here in tiles(width):
            total = own[:, here]
            for r in (a, b, c):
                total = total + decode(r, j, here, width)
            first, second = total[:rows], total[rows:]
            keep[:, here] = jnp.where(swapped, second, first)
            coded, scale = encode(jnp.where(swapped, first, second))
            scales.append(scale)
            put(send, here, coded, scales, width)


def fold(swap, *groups):
    vmem = pl.BlockSpec(memory_space=pltpu.VMEM)
    rows = groups[0][0].shape[0] // 2
    out_shape = [jax.ShapeDtypeStruct((rows, group[0].shape[1]), jnp.float32) for group in groups]
    out_shape.append(jax.ShapeDtypeStruct((rows, sum(group[1].shape[1] for group in groups)), jnp.bfloat16))
    return pl.pallas_call(
        fold_kernel,
        in_specs=[pl.BlockSpec(memory_space=pltpu.SMEM)] + [vmem] * (4 * len(groups)),
        out_specs=[vmem] * len(out_shape),
        out_shape=out_shape,
        cost_estimate=pl.CostEstimate(flops=1, bytes_accessed=1, transcendentals=0),
        name="fold",
    )(swap, *(array for group in groups for array in group))


def finish_kernel(keep0, keep1, got, keep2, got2, out, total):
    cut = got.shape[1] - got2.shape[1]
    got0, got1 = got.at[:, pl.ds(0, cut)], got.at[:, pl.ds(cut, got2.shape[1])]
    rows, width = keep0.shape
    for j, here in tiles(width):
        total[:rows, here] = keep0[:, here] + decode(got0, j, here, width)
    halves = []
    for keep, got in ((keep1, got1), (keep2, got2)):
        for j, here in tiles(keep.shape[1]):
            halves.append(keep[:, here] + decode(got, j, here, keep.shape[1]))
    total[rows:, :] = jnp.concatenate(halves, axis=1)
    for at in range(0, width, 256):
        here = slice(at, min(at + 256, width))
        out[here, :] = total[:, here].T.astype(out.dtype)


def finish(*keeps_and_gots):
    vmem = pl.BlockSpec(memory_space=pltpu.VMEM)
    keep0, keep1 = keeps_and_gots[:2]
    shape = (keep0.shape[0] + keep1.shape[0], keep0.shape[1])
    return pl.pallas_call(
        finish_kernel,
        in_specs=[vmem] * 5,
        out_specs=vmem,
        out_shape=jax.ShapeDtypeStruct(shape[::-1], jnp.bfloat16),
        scratch_shapes=[pltpu.VMEM(shape, jnp.float32)],
        name="finish",
    )(*keeps_and_gots)


def ahead(array, axis, step):
    n = SIZES[AXES.index(axis)]
    return lax.ppermute(array, axis, [(i, (i + step) % n) for i in range(n)])


def across(array, axis, bit):
    n = SIZES[AXES.index(axis)]
    return lax.ppermute(array, axis, [(i, i ^ bit) for i in range(n)])


def after(array, *others):
    return lax.optimization_barrier((array, *others))[0]


def phase(*arrays):
    return lax.optimization_barrier(arrays)


PARTS = (64, 64)


def on_device(inputs, cotangent, weight, adapter_down_factor, adapter_up_factor):
    y, xl, core, z, xh = (lax.axis_index(a) for a in AXES)
    row_position = (y * 2 + xl) * 2 + core
    column_position = z * 2 + xh
    tokens, hidden = cotangent.shape
    width_row_block = inputs.shape[1]
    width = weight.shape[0]
    rows = tokens // 2
    p = rows * PARTS[0] // sum(PARTS)
    q = rows - p
    base = jnp.reshape(lax.rem(z - y + 4, 4), (1,)).astype(jnp.int32)
    swap = jnp.reshape(xl ^ xh, (1,)).astype(jnp.int32)

    mine = lax.dynamic_slice_in_dim(cotangent, core * rows, rows, 0)
    theirs = lax.dynamic_slice_in_dim(cotangent, (1 - core) * rows, rows, 0)
    other = across(theirs, "core", 1)
    block = jnp.concatenate([mine, other], axis=1)

    up_own = lax.dynamic_slice_in_dim(adapter_up_factor, row_position * hidden, hidden, 1)
    up_other = lax.dynamic_slice_in_dim(adapter_up_factor, (row_position ^ 1) * hidden, hidden, 1)
    down_columns = scaling * lax.dynamic_slice_in_dim(adapter_down_factor.T, column_position * width, width, 1)
    down3 = jnp.concatenate([down_columns] * 3, axis=0)
    down_rows = lax.dynamic_slice_in_dim(adapter_down_factor, row_position * width_row_block, width_row_block, 0)

    low_part = dot_t(up_own, after(cotangent, other))
    proj_part = lax.dot_general(down_rows, inputs, (((0,), (1,)), ((), ())), preferred_element_type=jnp.float32)
    rank = low_part.shape[0]
    small = jnp.concatenate([low_part, proj_part], axis=0)

    up1, down1 = ahead(block[:p], "z", 1), ahead(block[:p], "z", 3)
    far1 = ahead(block[:p], "z", 2)
    x0, x1 = across(block[:p], "xh", 1), across(block[p:], "xh", 1)
    block, weight, up1, down1, far1, x0, x1, small = phase(block, weight, up1, down1, far1, x0, x1, small)

    up2, down2 = ahead(x0, "z", 1), ahead(x0, "z", 3)
    far2 = across(far1, "xh", 1)
    weight_other = across(weight, "core", 1)
    pair1 = jnp.concatenate([block[p:], x1], axis=0)
    small = small + across(small, "core", 1)
    small = small + across(small, "y", 1)
    small_other = across(small, "y", 2)
    block, up2, down2, far2, weight_other, pair1, small, small_other, up_other, down3 = phase(
        block, up2, down2, far2, weight_other, pair1, small, small_other, up_other, down3
    )
    small = small + small_other

    up4, down4 = ahead(pair1, "z", 1), ahead(pair1, "z", 3)
    layout0 = [(i, 0, p, step, i % 2 * p) for i, step in enumerate((0, 0, 3, 3, 1, 1, 2, 2))]
    kept0, a0, b0, c0 = partial(
        base, (block, x0, up1, up2, down1, down2, far1, far2), layout0, weight, weight_other, up_own, up_other, down3
    )
    small_other = across(small, "xl", 1)
    up4, down4, kept0, a0, b0, c0, small, small_other = phase(up4, down4, kept0, a0, b0, c0, small, small_other)
    small = small + small_other

    up5, down5 = ahead(up4[:q], "z", 1), ahead(down4[q:], "z", 3)
    a0, c0 = ahead(a0, "y", 1), ahead(c0, "y", 3)
    low48 = jnp.concatenate(pieces3(scaling * small[:rank]), axis=0)
    proj48 = jnp.concatenate(pieces3(scaling * small[rank:]), axis=0)

    def three(left, right):
        out = jnp.dot(left, right, preferred_element_type=jnp.float32)
        return out[:rank] + (out[rank : 2 * rank] + out[2 * rank :])

    parts = jnp.concatenate([three(low48, inputs), three(proj48, cotangent)], axis=1)
    parts_other = across(parts, "xh", 1)
    up5, down5, a0, c0, b0, parts, parts_other = phase(up5, down5, a0, c0, b0, parts, parts_other)
    parts = parts + parts_other

    layout1 = [
        (0, p, q, 0, 0),
        (1, 0, q, 0, q),
        (2, 0, 2 * q, 3, 0),
        (3, 0, 2 * q, 1, 0),
        (4, 0, q, 2, 0),
        (5, 0, q, 2, q),
    ]

    def half_of_sums(which, *given):
        return partial_half(
            which, base, (block, x1, up4, down4, up5, down5), layout1, weight, weight_other, given, down3
        )

    b0 = ahead(b0, "y", 2)
    kept1, a1, b1, c1, factors = half_of_sums(0, up_own, up_other)
    kept1, a1, b1, c1, b0, parts, block, factors = phase(kept1, a1, b1, c1, b0, parts, block, factors)

    a1, c1, b1 = ahead(a1, "y", 1), ahead(c1, "y", 3), ahead(b1, "y", 2)
    parts_other = across(parts, "z", 1)
    kept2, a2, b2, c2, _ = half_of_sums(1, factors)
    kept2, a2, b2, c2, a1, c1, b1, b0, parts_other = phase(kept2, a2, b2, c2, a1, c1, b1, b0, parts_other)
    parts = parts + parts_other

    a2, c2, b2 = ahead(a2, "y", 1), ahead(c2, "y", 3), ahead(b2, "y", 2)
    parts_other = across(parts, "z", 2)
    keep0, keep1, send1 = fold(swap, (kept0, a0, c0, b0), (kept1, a1, c1, b1))
    a2, c2, b2, keep0, keep1, send1, parts_other = phase(a2, c2, b2, keep0, keep1, send1, parts_other)

    got1 = across(send1, "xl", 1)
    keep2, send2 = fold(swap, (kept2, a2, c2, b2))
    got2 = across(send2, "xl", 1)
    parts = after(parts, send2) + parts_other
    grad_a = parts[:, :width_row_block].T
    grad_b = parts[:, width_row_block:]
    got1, got2, grad_a, grad_b = phase(got1, got2, grad_a, grad_b)
    grad_input = finish(keep0, keep1, got1, keep2, got2).T
    return grad_input, grad_a, grad_b


def solution(mesh):
    fine = Mesh(mesh.devices.reshape(SIZES), AXES)
    in_specs = (P(COL, ROW), P(COL, ROW), P(COL, ROW), P(), P())
    out_specs = (P(ROW, COL), P(ROW, None), P(None, ROW))
    return jax.shard_map(on_device, mesh=fine, in_specs=in_specs, out_specs=out_specs, check_vma=False)
```

```python
import functools

import jax
import jax.numpy as jnp
from jax import lax
from jax.experimental import pallas as pl
from jax.experimental.pallas import tpu as pltpu
from jax.sharding import Mesh, PartitionSpec as P

scaling = 2.0
AXES = ("y", "xl", "core", "z", "xh")
SIZES = (4, 2, 2, 4, 2)
ROW = ("y", "xl", "core")
COL = ("z", "xh")

POWER = 17
REACH = 170.0
SMALLEST = 1e-35
TILE = 512
KERNEL_BYTES = 58 << 20
ESTIMATED_FLOPS = 3000000000


def tiles(width):
    return [(j, slice(at, min(at + TILE, width))) for j, at in enumerate(range(0, width, TILE))]


def encode(value):
    largest = jnp.max(jnp.abs(value), axis=1, keepdims=True)
    scale = jnp.maximum(largest * 1.01, SMALLEST).astype(jnp.bfloat16).astype(jnp.float32)
    a = value * (REACH / scale)
    a2 = a * a
    a4 = a2 * a2
    a8 = a4 * a4
    return a8 * a8 * a, scale


def put(out, here, coded, scales, width):
    if here.stop < width:
        out[:, here] = coded.astype(jnp.bfloat16)
        return
    coded = jnp.concatenate([coded, jnp.zeros((coded.shape[0], out.shape[1] - width), jnp.float32)], axis=1)
    column = lax.broadcasted_iota(jnp.int32, coded.shape, 1) + here.start
    for j, scale in enumerate(scales):
        coded = jnp.where(column == width + j, scale, coded)
    out[:, here.start :] = coded.astype(jnp.bfloat16)


def decode(ref, j, here, width, rows=slice(None)):
    coded = ref[rows, here].astype(jnp.float32)
    scale = ref[rows, width + j : width + j + 1].astype(jnp.float32) * (1.0 / REACH)
    size = jnp.abs(coded)
    root = jnp.where(size > 0.0, jnp.exp(jnp.log(size) * (1.0 / POWER)), 0.0)
    return jnp.where(coded < 0.0, -root, root) * scale


def split3(value):
    high = value.astype(jnp.bfloat16)
    rest = value - high.astype(jnp.float32)
    middle = rest.astype(jnp.bfloat16)
    low = (rest - middle.astype(jnp.float32)).astype(jnp.bfloat16)
    return high, middle, low


def pieces3(value):
    high = lax.reduce_precision(value, 8, 7)
    middle = lax.reduce_precision(value - high, 8, 7)
    return [p.astype(jnp.bfloat16) for p in (high, middle, value - high - middle)]


def dot(left, right):
    return jnp.dot(left, right, preferred_element_type=jnp.float32)


def dot_t(left, right):
    return lax.dot_general(
        left, right, (((1,), (1,)), ((), ())), preferred_element_type=jnp.float32
    )


def partial_kernel(width, layout, n, base, *refs):
    pieces, (wo, wr, uo, ur, down, own, *outs, held, low, kept_scales, sems) = refs[:n], refs[n:]
    j = pl.program_id(0)
    rows = own.shape[0]
    half = wo.shape[1]
    full = width // TILE
    rest = width - full * TILE
    tail = own.shape[1] // 128 * 128
    column = lax.broadcasted_iota(jnp.int32, (rows, 128), 1)

    @pl.when(j == 0)
    def _():
        gathers = []
        for i, (which, start, size, step, offset) in enumerate(layout):
            at = pl.multiple_of(lax.rem(base[0] + step, 4) * rows + offset, 16)
            gathers.append(pltpu.make_async_copy(pieces[which].at[pl.ds(start, size)], held.at[pl.ds(at, size)], sems.at[i]))
            gathers[-1].start()
        for copy in gathers:
            copy.wait()
        total = dot_t(held[:, :half], uo[...]) + dot_t(held[:, half:], ur[...])
        low[...] = jnp.concatenate(split3(total), axis=1)
        kept_scales[...] = jnp.zeros_like(kept_scales)

    def sums(size):
        value = dot_t(held[:, :half], wo[:size, :]) + dot_t(held[:, half:], wr[:size, :]) + dot(low[...], down[:, :size])
        for d in range(3):
            coded, scale = encode(value[(d + 1) * rows : (d + 2) * rows])
            kept_scales[d] = jnp.where(column == width % 128 + j, scale, kept_scales[d])
            yield value, d, coded

    @pl.when(j < full)
    def _():
        here = pl.ds(pl.multiple_of(j * TILE, TILE), TILE)
        for value, d, coded in sums(TILE):
            outs[d][:, here] = coded.astype(jnp.bfloat16)
        own[:, here] = value[:rows]

    @pl.when(j == full)
    def _():
        for value, d, coded in sums(rest):
            before = tail - full * TILE
            outs[d][:, full * TILE : tail] = coded[:, :before].astype(jnp.bfloat16)
            last = jnp.concatenate([coded[:, before:], jnp.zeros((rows, 128 - (width - tail)), jnp.float32)], axis=1)
            outs[d][:, tail:] = jnp.where(column < width - tail, last, kept_scales[d]).astype(jnp.bfloat16)
        own[:, full * TILE :] = value[:rows]


def partial(base, pieces, layout, wo, wr, uo, ur, down):
    width, half = wo.shape
    rows = sum(size for _, _, size, _, _ in layout) // 4
    padded = (width // 128 + 1) * 128
    hbm = pl.BlockSpec(memory_space=pltpu.HBM)
    strip = lambda a: pl.BlockSpec((TILE, a.shape[1]), lambda j, b: (j, 0))
    whole = lambda a: pl.BlockSpec(a.shape, lambda j, b: (0, 0))
    return pl.pallas_call(
        functools.partial(partial_kernel, width, layout, len(pieces)),
        grid_spec=pltpu.PrefetchScalarGridSpec(
            num_scalar_prefetch=1,
            grid=(width // TILE + 1,),
            in_specs=[hbm] * len(pieces) + [
                strip(wo),
                strip(wr),
                whole(uo),
                whole(ur),
                pl.BlockSpec((down.shape[0], TILE), lambda j, b: (0, j)),
            ],
            out_specs=[pl.BlockSpec((rows, width), lambda j, b: (0, 0))]
            + [pl.BlockSpec((rows, padded), lambda j, b: (0, 0))] * 3,
            scratch_shapes=[
                pltpu.VMEM((4 * rows, 2 * half), jnp.bfloat16),
                pltpu.VMEM((4 * rows, 48), jnp.bfloat16),
                pltpu.VMEM((3, rows, 128), jnp.float32),
                pltpu.SemaphoreType.DMA((len(layout),)),
            ],
        ),
        out_shape=[jax.ShapeDtypeStruct((rows, width), jnp.float32)]
        + [jax.ShapeDtypeStruct((rows, padded), jnp.bfloat16)] * 3,
        compiler_params=pltpu.CompilerParams(vmem_limit_bytes=KERNEL_BYTES),
        cost_estimate=pl.CostEstimate(flops=ESTIMATED_FLOPS, bytes_accessed=1, transcendentals=0),
        name="partial",
    )(base, *pieces, wo, wr, uo, ur, down)


def half_kernel(which, width, layout, n, base, *refs):
    pieces, (wo, wr, *given), refs = refs[:n], refs[n:-12], refs[-12:]
    down, own, *outs, low, held, held_wo, held_wr, total, sems, w_sems = refs
    rows = own.shape[0]
    half = wo.shape[1]
    always = base[0] >= 0
    strip = pl.ds(which * width, width)
    first = pltpu.make_async_copy(wo.at[strip], held_wo, w_sems.at[0])
    second = pltpu.make_async_copy(wr.at[strip], held_wr, w_sems.at[1])
    gathers = []
    for i, (piece, start, size, step, offset) in enumerate(layout):
        at = pl.multiple_of(lax.rem(base[0] + step, 4) * rows + offset, 16)
        gathers.append(pltpu.make_async_copy(pieces[piece].at[pl.ds(start, size)], held.at[pl.ds(at, size)], sems.at[i]))
        gathers[-1].start()
    first.start()
    second.start()

    @pl.when(always)
    def _():
        for copy in gathers:
            copy.wait()
        if len(given) == 1:
            low[...] = given[0][...]
        else:
            factors = dot_t(held[:, :half], given[0][...]) + dot_t(held[:, half:], given[1][...])
            low[...] = jnp.concatenate(split3(factors), axis=1)

    @pl.when(always)
    def _():
        first.wait()
        for _, here in tiles(width):
            shift = slice(which * width + here.start, which * width + here.stop)
            total[:, here] = dot_t(held[:, :half], held_wo[here, :]) + dot(low[...], down[:, shift])

    @pl.when(always)
    def _():
        second.wait()
        scales = [[], [], []]
        for j, here in tiles(width):
            value = total[:, here] + dot_t(held[:, half:], held_wr[here, :])
            own[:, here] = value[:rows]
            for d, out in enumerate(outs):
                coded, scale = encode(value[(d + 1) * rows : (d + 2) * rows])
                scales[d].append(scale)
                put(out, here, coded, scales[d], width)


def partial_half(which, base, pieces, layout, wo, wr, given, down):
    width, half = wo.shape[0] // 2, wo.shape[1]
    rows = sum(size for _, _, size, _, _ in layout) // 4
    padded = (width // 128 + 1) * 128
    hbm = pl.BlockSpec(memory_space=pltpu.HBM)
    whole = lambda a: pl.BlockSpec(a.shape, lambda j, b: (0, 0))
    return pl.pallas_call(
        functools.partial(half_kernel, which, width, layout, len(pieces)),
        grid_spec=pltpu.PrefetchScalarGridSpec(
            num_scalar_prefetch=1,
            grid=(1,),
            in_specs=[hbm] * (len(pieces) + 2) + [whole(g) for g in given] + [whole(down)],
            out_specs=[pl.BlockSpec((rows, width), lambda j, b: (0, 0))]
            + [pl.BlockSpec((rows, padded), lambda j, b: (0, 0))] * 3
            + [pl.BlockSpec((4 * rows, 48), lambda j, b: (0, 0))],
            scratch_shapes=[
                pltpu.VMEM((4 * rows, 2 * half), jnp.bfloat16),
                pltpu.VMEM((width, half), jnp.bfloat16),
                pltpu.VMEM((width, half), jnp.bfloat16),
                pltpu.VMEM((4 * rows, width), jnp.float32),
                pltpu.SemaphoreType.DMA((len(layout),)),
                pltpu.SemaphoreType.DMA((2,)),
            ],
        ),
        out_shape=[jax.ShapeDtypeStruct((rows, width), jnp.float32)]
        + [jax.ShapeDtypeStruct((rows, padded), jnp.bfloat16)] * 3
        + [jax.ShapeDtypeStruct((4 * rows, 48), jnp.bfloat16)],
        compiler_params=pltpu.CompilerParams(vmem_limit_bytes=KERNEL_BYTES),
        cost_estimate=pl.CostEstimate(flops=ESTIMATED_FLOPS, bytes_accessed=1, transcendentals=0),
        name="partial_half",
    )(base, *pieces, wo, wr, *given, down)


def fold_kernel(*refs):
    swapped = refs[0][0] == 1
    n = (len(refs) - 2) // 5
    at = 0
    for i in range(n):
        own, a, b, c = refs[1 + 4 * i : 5 + 4 * i]
        keep, send = refs[1 + 4 * n + i], refs[-1].at[:, pl.ds(at, a.shape[1])]
        at += a.shape[1]
        rows, width = keep.shape
        scales = []
        for j, here in tiles(width):
            total = own[:, here]
            for r in (a, b, c):
                total = total + decode(r, j, here, width)
            first, second = total[:rows], total[rows:]
            keep[:, here] = jnp.where(swapped, second, first)
            coded, scale = encode(jnp.where(swapped, first, second))
            scales.append(scale)
            put(send, here, coded, scales, width)


def fold(swap, *groups):
    vmem = pl.BlockSpec(memory_space=pltpu.VMEM)
    rows = groups[0][0].shape[0] // 2
    out_shape = [jax.ShapeDtypeStruct((rows, group[0].shape[1]), jnp.float32) for group in groups]
    out_shape.append(jax.ShapeDtypeStruct((rows, sum(group[1].shape[1] for group in groups)), jnp.bfloat16))
    return pl.pallas_call(
        fold_kernel,
        in_specs=[pl.BlockSpec(memory_space=pltpu.SMEM)] + [vmem] * (4 * len(groups)),
        out_specs=[vmem] * len(out_shape),
        out_shape=out_shape,
        cost_estimate=pl.CostEstimate(flops=1, bytes_accessed=1, transcendentals=0),
        name="fold",
    )(swap, *(array for group in groups for array in group))


def finish_kernel(keep0, keep1, got, keep2, got2, out, total):
    cut = got.shape[1] - got2.shape[1]
    got0, got1 = got.at[:, pl.ds(0, cut)], got.at[:, pl.ds(cut, got2.shape[1])]
    rows, width = keep0.shape
    for j, here in tiles(width):
        total[:rows, here] = keep0[:, here] + decode(got0, j, here, width)
    halves = []
    for keep, got in ((keep1, got1), (keep2, got2)):
        for j, here in tiles(keep.shape[1]):
            halves.append(keep[:, here] + decode(got, j, here, keep.shape[1]))
    total[rows:, :] = jnp.concatenate(halves, axis=1)
    for at in range(0, width, 256):
        here = slice(at, min(at + 256, width))
        out[here, :] = total[:, here].T.astype(out.dtype)


def finish(*keeps_and_gots):
    vmem = pl.BlockSpec(memory_space=pltpu.VMEM)
    keep0, keep1 = keeps_and_gots[:2]
    shape = (keep0.shape[0] + keep1.shape[0], keep0.shape[1])
    return pl.pallas_call(
        finish_kernel,
        in_specs=[vmem] * 5,
        out_specs=vmem,
        out_shape=jax.ShapeDtypeStruct(shape[::-1], jnp.bfloat16),
        scratch_shapes=[pltpu.VMEM(shape, jnp.float32)],
        name="finish",
    )(*keeps_and_gots)


def ahead(array, axis, step):
    n = SIZES[AXES.index(axis)]
    return lax.ppermute(array, axis, [(i, (i + step) % n) for i in range(n)])


def across(array, axis, bit):
    n = SIZES[AXES.index(axis)]
    return lax.ppermute(array, axis, [(i, i ^ bit) for i in range(n)])


def after(array, *others):
    return lax.optimization_barrier((array, *others))[0]


def phase(*arrays):
    return lax.optimization_barrier(arrays)


PARTS = (64, 64)


def on_device(inputs, cotangent, weight, adapter_down_factor, adapter_up_factor):
    y, xl, core, z, xh = (lax.axis_index(a) for a in AXES)
    row_position = (y * 2 + xl) * 2 + core
    column_position = z * 2 + xh
    tokens, hidden = cotangent.shape
    width_row_block = inputs.shape[1]
    width = weight.shape[0]
    rows = tokens // 2
    p = rows * PARTS[0] // sum(PARTS)
    q = rows - p
    base = jnp.reshape(lax.rem(z - y + 4, 4), (1,)).astype(jnp.int32)
    swap = jnp.reshape(xl ^ xh, (1,)).astype(jnp.int32)

    mine = lax.dynamic_slice_in_dim(cotangent, core * rows, rows, 0)
    theirs = lax.dynamic_slice_in_dim(cotangent, (1 - core) * rows, rows, 0)
    other = across(theirs, "core", 1)
    block = jnp.concatenate([mine, other], axis=1)

    up_own = lax.dynamic_slice_in_dim(adapter_up_factor, row_position * hidden, hidden, 1)
    up_other = lax.dynamic_slice_in_dim(adapter_up_factor, (row_position ^ 1) * hidden, hidden, 1)
    down_columns = scaling * lax.dynamic_slice_in_dim(adapter_down_factor.T, column_position * width, width, 1)
    down3 = jnp.concatenate([down_columns] * 3, axis=0)
    down_rows = lax.dynamic_slice_in_dim(adapter_down_factor, row_position * width_row_block, width_row_block, 0)

    low_part = dot_t(up_own, after(cotangent, other))
    proj_part = lax.dot_general(down_rows, inputs, (((0,), (1,)), ((), ())), preferred_element_type=jnp.float32)
    rank = low_part.shape[0]
    small = jnp.concatenate([low_part, proj_part], axis=0)

    up1, down1 = ahead(block[:p], "z", 1), ahead(block[:p], "z", 3)
    far1 = ahead(block[:p], "z", 2)
    x0, x1 = across(block[:p], "xh", 1), across(block[p:], "xh", 1)
    block, weight, up1, down1, far1, x0, x1, small = phase(block, weight, up1, down1, far1, x0, x1, small)

    up2, down2 = ahead(x0, "z", 1), ahead(x0, "z", 3)
    far2 = across(far1, "xh", 1)
    weight_other = across(weight, "core", 1)
    pair1 = jnp.concatenate([block[p:], x1], axis=0)
    small = small + across(small, "core", 1)
    small = small + across(small, "y", 1)
    small_other = across(small, "y", 2)
    block, up2, down2, far2, weight_other, pair1, small, small_other, up_other, down3 = phase(
        block, up2, down2, far2, weight_other, pair1, small, small_other, up_other, down3
    )
    small = small + small_other

    up4, down4 = ahead(pair1, "z", 1), ahead(pair1, "z", 3)
    layout0 = [(i, 0, p, step, i % 2 * p) for i, step in enumerate((0, 0, 3, 3, 1, 1, 2, 2))]
    kept0, a0, b0, c0 = partial(
        base, (block, x0, up1, up2, down1, down2, far1, far2), layout0, weight, weight_other, up_own, up_other, down3
    )
    small_other = across(small, "xl", 1)
    up4, down4, kept0, a0, b0, c0, small, small_other = phase(up4, down4, kept0, a0, b0, c0, small, small_other)
    small = small + small_other

    up5, down5 = ahead(up4[:q], "z", 1), ahead(down4[q:], "z", 3)
    a0, c0 = ahead(a0, "y", 1), ahead(c0, "y", 3)
    low48 = jnp.concatenate(pieces3(scaling * small[:rank]), axis=0)
    proj48 = jnp.concatenate(pieces3(scaling * small[rank:]), axis=0)

    def three(left, right):
        out = jnp.dot(left, right, preferred_element_type=jnp.float32)
        return out[:rank] + (out[rank : 2 * rank] + out[2 * rank :])

    parts = jnp.concatenate([three(low48, inputs), three(proj48, cotangent)], axis=1)
    parts_other = across(parts, "xh", 1)
    up5, down5, a0, c0, b0, parts, parts_other = phase(up5, down5, a0, c0, b0, parts, parts_other)
    parts = parts + parts_other

    layout1 = [
        (0, p, q, 0, 0),
        (1, 0, q, 0, q),
        (2, 0, 2 * q, 3, 0),
        (3, 0, 2 * q, 1, 0),
        (4, 0, q, 2, 0),
        (5, 0, q, 2, q),
    ]

    def half_of_sums(which, *given):
        return partial_half(
            which, base, (block, x1, up4, down4, up5, down5), layout1, weight, weight_other, given, down3
        )

    b0 = ahead(b0, "y", 2)
    kept1, a1, b1, c1, factors = half_of_sums(0, up_own, up_other)
    kept1, a1, b1, c1, b0, parts, block, factors = phase(kept1, a1, b1, c1, b0, parts, block, factors)

    a1, c1, b1 = ahead(a1, "y", 1), ahead(c1, "y", 3), ahead(b1, "y", 2)
    parts_other = across(parts, "z", 1)
    kept2, a2, b2, c2, _ = half_of_sums(1, factors)
    kept2, a2, b2, c2, a1, c1, b1, b0, parts_other = phase(kept2, a2, b2, c2, a1, c1, b1, b0, parts_other)
    parts = parts + parts_other

    a2, c2, b2 = ahead(a2, "y", 1), ahead(c2, "y", 3), ahead(b2, "y", 2)
    parts_other = across(parts, "z", 2)
    keep0, keep1, send1 = fold(swap, (kept0, a0, c0, b0), (kept1, a1, c1, b1))
    a2, c2, b2, keep0, keep1, send1, parts_other = phase(a2, c2, b2, keep0, keep1, send1, parts_other)

    got1 = across(send1, "xl", 1)
    keep2, send2 = fold(swap, (kept2, a2, c2, b2))
    got2 = across(send2, "xl", 1)
    parts = after(parts, send2) + parts_other
    grad_a = parts[:, :width_row_block].T
    grad_b = parts[:, width_row_block:]
    got1, got2, grad_a, grad_b = phase(got1, got2, grad_a, grad_b)
    grad_input = finish(keep0, keep1, got1, keep2, got2).T
    return grad_input, grad_a, grad_b


def solution(mesh):
    fine = Mesh(mesh.devices.reshape(SIZES), AXES)
    in_specs = (P(COL, ROW), P(COL, ROW), P(COL, ROW), P(), P())
    out_specs = (P(ROW, COL), P(ROW, None), P(None, ROW))
    return jax.shard_map(on_device, mesh=fine, in_specs=in_specs, out_specs=out_specs, check_vma=False)
```

```python
import functools

import jax
import jax.numpy as jnp
from jax import lax
from jax.experimental import pallas as pl
from jax.experimental.pallas import tpu as pltpu
from jax.sharding import Mesh, PartitionSpec as P

scaling = 2.0
AXES = ("y", "xl", "core", "z", "xh")
SIZES = (4, 2, 2, 4, 2)
ROW = ("y", "xl", "core")
COL = ("z", "xh")

POWER = 17
REACH = 170.0
SMALLEST = 1e-35
TILE = 512
KERNEL_BYTES = 58 << 20
ESTIMATED_FLOPS = 3000000000


def tiles(width):
    return [(j, slice(at, min(at + TILE, width))) for j, at in enumerate(range(0, width, TILE))]


def encode(value):
    largest = jnp.max(jnp.abs(value), axis=1, keepdims=True)
    scale = jnp.maximum(largest * 1.01, SMALLEST).astype(jnp.bfloat16).astype(jnp.float32)
    a = value * (REACH / scale)
    a2 = a * a
    a4 = a2 * a2
    a8 = a4 * a4
    return a8 * a8 * a, scale


def put(out, here, coded, scales, width):
    if here.stop < width:
        out[:, here] = coded.astype(jnp.bfloat16)
        return
    coded = jnp.concatenate([coded, jnp.zeros((coded.shape[0], out.shape[1] - width), jnp.float32)], axis=1)
    column = lax.broadcasted_iota(jnp.int32, coded.shape, 1) + here.start
    for j, scale in enumerate(scales):
        coded = jnp.where(column == width + j, scale, coded)
    out[:, here.start :] = coded.astype(jnp.bfloat16)


def decode(ref, j, here, width, rows=slice(None)):
    coded = ref[rows, here].astype(jnp.float32)
    scale = ref[rows, width + j : width + j + 1].astype(jnp.float32) * (1.0 / REACH)
    size = jnp.abs(coded)
    root = jnp.where(size > 0.0, jnp.exp(jnp.log(size) * (1.0 / POWER)), 0.0)
    return jnp.where(coded < 0.0, -root, root) * scale


def split3(value):
    high = value.astype(jnp.bfloat16)
    rest = value - high.astype(jnp.float32)
    middle = rest.astype(jnp.bfloat16)
    low = (rest - middle.astype(jnp.float32)).astype(jnp.bfloat16)
    return high, middle, low


def pieces3(value):
    high = lax.reduce_precision(value, 8, 7)
    middle = lax.reduce_precision(value - high, 8, 7)
    return [p.astype(jnp.bfloat16) for p in (high, middle, value - high - middle)]


def dot(left, right):
    return jnp.dot(left, right, preferred_element_type=jnp.float32)


def dot_t(left, right):
    return lax.dot_general(
        left, right, (((1,), (1,)), ((), ())), preferred_element_type=jnp.float32
    )


def partial_kernel(width, layout, n, base, *refs):
    pieces, (wo, wr, uo, ur, down, own, *outs, held, low, kept_scales, sems) = refs[:n], refs[n:]
    j = pl.program_id(0)
    rows = own.shape[0]
    half = wo.shape[1]
    full = width // TILE
    rest = width - full * TILE
    tail = own.shape[1] // 128 * 128
    column = lax.broadcasted_iota(jnp.int32, (rows, 128), 1)

    @pl.when(j == 0)
    def _():
        gathers = []
        for i, (which, start, size, step, offset) in enumerate(layout):
            at = pl.multiple_of(lax.rem(base[0] + step, 4) * rows + offset, 16)
            gathers.append(pltpu.make_async_copy(pieces[which].at[pl.ds(start, size)], held.at[pl.ds(at, size)], sems.at[i]))
            gathers[-1].start()
        for copy in gathers:
            copy.wait()
        total = dot_t(held[:, :half], uo[...]) + dot_t(held[:, half:], ur[...])
        low[...] = jnp.concatenate(split3(total), axis=1)
        kept_scales[...] = jnp.zeros_like(kept_scales)

    def sums(size):
        value = dot_t(held[:, :half], wo[:size, :]) + dot_t(held[:, half:], wr[:size, :]) + dot(low[...], down[:, :size])
        for d in range(3):
            coded, scale = encode(value[(d + 1) * rows : (d + 2) * rows])
            kept_scales[d] = jnp.where(column == width % 128 + j, scale, kept_scales[d])
            yield value, d, coded

    @pl.when(j < full)
    def _():
        here = pl.ds(pl.multiple_of(j * TILE, TILE), TILE)
        for value, d, coded in sums(TILE):
            outs[d][:, here] = coded.astype(jnp.bfloat16)
        own[:, here] = value[:rows]

    @pl.when(j == full)
    def _():
        for value, d, coded in sums(rest):
            before = tail - full * TILE
            outs[d][:, full * TILE : tail] = coded[:, :before].astype(jnp.bfloat16)
            last = jnp.concatenate([coded[:, before:], jnp.zeros((rows, 128 - (width - tail)), jnp.float32)], axis=1)
            outs[d][:, tail:] = jnp.where(column < width - tail, last, kept_scales[d]).astype(jnp.bfloat16)
        own[:, full * TILE :] = value[:rows]


def partial(base, pieces, layout, wo, wr, uo, ur, down):
    width, half = wo.shape
    rows = sum(size for _, _, size, _, _ in layout) // 4
    padded = (width // 128 + 1) * 128
    hbm = pl.BlockSpec(memory_space=pltpu.HBM)
    strip = lambda a: pl.BlockSpec((TILE, a.shape[1]), lambda j, b: (j, 0))
    whole = lambda a: pl.BlockSpec(a.shape, lambda j, b: (0, 0))
    return pl.pallas_call(
        functools.partial(partial_kernel, width, layout, len(pieces)),
        grid_spec=pltpu.PrefetchScalarGridSpec(
            num_scalar_prefetch=1,
            grid=(width // TILE + 1,),
            in_specs=[hbm] * len(pieces) + [
                strip(wo),
                strip(wr),
                whole(uo),
                whole(ur),
                pl.BlockSpec((down.shape[0], TILE), lambda j, b: (0, j)),
            ],
            out_specs=[pl.BlockSpec((rows, width), lambda j, b: (0, 0))]
            + [pl.BlockSpec((rows, padded), lambda j, b: (0, 0))] * 3,
            scratch_shapes=[
                pltpu.VMEM((4 * rows, 2 * half), jnp.bfloat16),
                pltpu.VMEM((4 * rows, 48), jnp.bfloat16),
                pltpu.VMEM((3, rows, 128), jnp.float32),
                pltpu.SemaphoreType.DMA((len(layout),)),
            ],
        ),
        out_shape=[jax.ShapeDtypeStruct((rows, width), jnp.float32)]
        + [jax.ShapeDtypeStruct((rows, padded), jnp.bfloat16)] * 3,
        compiler_params=pltpu.CompilerParams(vmem_limit_bytes=KERNEL_BYTES),
        cost_estimate=pl.CostEstimate(flops=ESTIMATED_FLOPS, bytes_accessed=1, transcendentals=0),
        name="partial",
    )(base, *pieces, wo, wr, uo, ur, down)


def half_kernel(which, width, layout, n, base, *refs):
    pieces, (wo, wr, *given), refs = refs[:n], refs[n:-12], refs[-12:]
    down, own, *outs, low, held, held_wo, held_wr, total, sems, w_sems = refs
    rows = own.shape[0]
    half = wo.shape[1]
    always = base[0] >= 0
    strip = pl.ds(which * width, width)
    first = pltpu.make_async_copy(wo.at[strip], held_wo, w_sems.at[0])
    second = pltpu.make_async_copy(wr.at[strip], held_wr, w_sems.at[1])
    gathers = []
    for i, (piece, start, size, step, offset) in enumerate(layout):
        at = pl.multiple_of(lax.rem(base[0] + step, 4) * rows + offset, 16)
        gathers.append(pltpu.make_async_copy(pieces[piece].at[pl.ds(start, size)], held.at[pl.ds(at, size)], sems.at[i]))
        gathers[-1].start()
    first.start()
    second.start()

    @pl.when(always)
    def _():
        for copy in gathers:
            copy.wait()
        if len(given) == 1:
            low[...] = given[0][...]
        else:
            factors = dot_t(held[:, :half], given[0][...]) + dot_t(held[:, half:], given[1][...])
            low[...] = jnp.concatenate(split3(factors), axis=1)

    @pl.when(always)
    def _():
        first.wait()
        for _, here in tiles(width):
            shift = slice(which * width + here.start, which * width + here.stop)
            total[:, here] = dot_t(held[:, :half], held_wo[here, :]) + dot(low[...], down[:, shift])

    @pl.when(always)
    def _():
        second.wait()
        scales = [[], [], []]
        for j, here in tiles(width):
            value = total[:, here] + dot_t(held[:, half:], held_wr[here, :])
            own[:, here] = value[:rows]
            for d, out in enumerate(outs):
                coded, scale = encode(value[(d + 1) * rows : (d + 2) * rows])
                scales[d].append(scale)
                put(out, here, coded, scales[d], width)


def partial_half(which, base, pieces, layout, wo, wr, given, down):
    width, half = wo.shape[0] // 2, wo.shape[1]
    rows = sum(size for _, _, size, _, _ in layout) // 4
    padded = (width // 128 + 1) * 128
    hbm = pl.BlockSpec(memory_space=pltpu.HBM)
    whole = lambda a: pl.BlockSpec(a.shape, lambda j, b: (0, 0))
    return pl.pallas_call(
        functools.partial(half_kernel, which, width, layout, len(pieces)),
        grid_spec=pltpu.PrefetchScalarGridSpec(
            num_scalar_prefetch=1,
            grid=(1,),
            in_specs=[hbm] * (len(pieces) + 2) + [whole(g) for g in given] + [whole(down)],
            out_specs=[pl.BlockSpec((rows, width), lambda j, b: (0, 0))]
            + [pl.BlockSpec((rows, padded), lambda j, b: (0, 0))] * 3
            + [pl.BlockSpec((4 * rows, 48), lambda j, b: (0, 0))],
            scratch_shapes=[
                pltpu.VMEM((4 * rows, 2 * half), jnp.bfloat16),
                pltpu.VMEM((width, half), jnp.bfloat16),
                pltpu.VMEM((width, half), jnp.bfloat16),
                pltpu.VMEM((4 * rows, width), jnp.float32),
                pltpu.SemaphoreType.DMA((len(layout),)),
                pltpu.SemaphoreType.DMA((2,)),
            ],
        ),
        out_shape=[jax.ShapeDtypeStruct((rows, width), jnp.float32)]
        + [jax.ShapeDtypeStruct((rows, padded), jnp.bfloat16)] * 3
        + [jax.ShapeDtypeStruct((4 * rows, 48), jnp.bfloat16)],
        compiler_params=pltpu.CompilerParams(vmem_limit_bytes=KERNEL_BYTES),
        cost_estimate=pl.CostEstimate(flops=ESTIMATED_FLOPS, bytes_accessed=1, transcendentals=0),
        name="partial_half",
    )(base, *pieces, wo, wr, *given, down)


def fold_kernel(*refs):
    swapped = refs[0][0] == 1
    n = (len(refs) - 2) // 5
    at = 0
    for i in range(n):
        own, a, b, c = refs[1 + 4 * i : 5 + 4 * i]
        keep, send = refs[1 + 4 * n + i], refs[-1].at[:, pl.ds(at, a.shape[1])]
        at += a.shape[1]
        rows, width = keep.shape
        scales = []
        for j, here in tiles(width):
            total = own[:, here]
            for r in (a, b, c):
                total = total + decode(r, j, here, width)
            first, second = total[:rows], total[rows:]
            keep[:, here] = jnp.where(swapped, second, first)
            coded, scale = encode(jnp.where(swapped, first, second))
            scales.append(scale)
            put(send, here, coded, scales, width)


def fold(swap, *groups):
    vmem = pl.BlockSpec(memory_space=pltpu.VMEM)
    rows = groups[0][0].shape[0] // 2
    out_shape = [jax.ShapeDtypeStruct((rows, group[0].shape[1]), jnp.float32) for group in groups]
    out_shape.append(jax.ShapeDtypeStruct((rows, sum(group[1].shape[1] for group in groups)), jnp.bfloat16))
    return pl.pallas_call(
        fold_kernel,
        in_specs=[pl.BlockSpec(memory_space=pltpu.SMEM)] + [vmem] * (4 * len(groups)),
        out_specs=[vmem] * len(out_shape),
        out_shape=out_shape,
        cost_estimate=pl.CostEstimate(flops=2000000000, bytes_accessed=1, transcendentals=0),
        name="fold",
    )(swap, *(array for group in groups for array in group))


def finish_kernel(keep0, keep1, got, keep2, got2, out, total):
    cut = got.shape[1] - got2.shape[1]
    got0, got1 = got.at[:, pl.ds(0, cut)], got.at[:, pl.ds(cut, got2.shape[1])]
    rows, width = keep0.shape
    for j, here in tiles(width):
        total[:rows, here] = keep0[:, here] + decode(got0, j, here, width)
    halves = []
    for keep, got in ((keep1, got1), (keep2, got2)):
        for j, here in tiles(keep.shape[1]):
            halves.append(keep[:, here] + decode(got, j, here, keep.shape[1]))
    total[rows:, :] = jnp.concatenate(halves, axis=1)
    for at in range(0, width, 256):
        here = slice(at, min(at + 256, width))
        out[here, :] = total[:, here].T.astype(out.dtype)


def finish(*keeps_and_gots):
    vmem = pl.BlockSpec(memory_space=pltpu.VMEM)
    keep0, keep1 = keeps_and_gots[:2]
    shape = (keep0.shape[0] + keep1.shape[0], keep0.shape[1])
    return pl.pallas_call(
        finish_kernel,
        in_specs=[vmem] * 5,
        out_specs=vmem,
        out_shape=jax.ShapeDtypeStruct(shape[::-1], jnp.bfloat16),
        scratch_shapes=[pltpu.VMEM(shape, jnp.float32)],
        name="finish",
    )(*keeps_and_gots)


def ahead(array, axis, step):
    n = SIZES[AXES.index(axis)]
    return lax.ppermute(array, axis, [(i, (i + step) % n) for i in range(n)])


def across(array, axis, bit):
    n = SIZES[AXES.index(axis)]
    return lax.ppermute(array, axis, [(i, i ^ bit) for i in range(n)])


def after(array, *others):
    return lax.optimization_barrier((array, *others))[0]


def phase(*arrays):
    return lax.optimization_barrier(arrays)


PARTS = (64, 64)


def on_device(inputs, cotangent, weight, adapter_down_factor, adapter_up_factor):
    y, xl, core, z, xh = (lax.axis_index(a) for a in AXES)
    row_position = (y * 2 + xl) * 2 + core
    column_position = z * 2 + xh
    tokens, hidden = cotangent.shape
    width_row_block = inputs.shape[1]
    width = weight.shape[0]
    rows = tokens // 2
    p = rows * PARTS[0] // sum(PARTS)
    q = rows - p
    base = jnp.reshape(lax.rem(z - y + 4, 4), (1,)).astype(jnp.int32)
    swap = jnp.reshape(xl ^ xh, (1,)).astype(jnp.int32)

    mine = lax.dynamic_slice_in_dim(cotangent, core * rows, rows, 0)
    theirs = lax.dynamic_slice_in_dim(cotangent, (1 - core) * rows, rows, 0)
    other = across(theirs, "core", 1)
    block = jnp.concatenate([mine, other], axis=1)

    up_own = lax.dynamic_slice_in_dim(adapter_up_factor, row_position * hidden, hidden, 1)
    up_other = lax.dynamic_slice_in_dim(adapter_up_factor, (row_position ^ 1) * hidden, hidden, 1)
    down_columns = scaling * lax.dynamic_slice_in_dim(adapter_down_factor.T, column_position * width, width, 1)
    down3 = jnp.concatenate([down_columns] * 3, axis=0)
    down_rows = lax.dynamic_slice_in_dim(adapter_down_factor, row_position * width_row_block, width_row_block, 0)

    low_part = dot_t(up_own, after(cotangent, other))
    proj_part = lax.dot_general(down_rows, inputs, (((0,), (1,)), ((), ())), preferred_element_type=jnp.float32)
    rank = low_part.shape[0]
    small = jnp.concatenate([low_part, proj_part], axis=0)

    up1, down1 = ahead(block[:p], "z", 1), ahead(block[:p], "z", 3)
    far1 = ahead(block[:p], "z", 2)
    x0, x1 = across(block[:p], "xh", 1), across(block[p:], "xh", 1)
    block, weight, up1, down1, far1, x0, x1, small = phase(block, weight, up1, down1, far1, x0, x1, small)

    up2, down2 = ahead(x0, "z", 1), ahead(x0, "z", 3)
    far2 = across(far1, "xh", 1)
    weight_other = across(weight, "core", 1)
    pair1 = jnp.concatenate([block[p:], x1], axis=0)
    small = small + across(small, "core", 1)
    small = small + across(small, "y", 1)
    small_other = across(small, "y", 2)
    block, up2, down2, far2, weight_other, pair1, small, small_other, up_other, down3 = phase(
        block, up2, down2, far2, weight_other, pair1, small, small_other, up_other, down3
    )
    small = small + small_other

    up4, down4 = ahead(pair1, "z", 1), ahead(pair1, "z", 3)
    layout0 = [(i, 0, p, step, i % 2 * p) for i, step in enumerate((0, 0, 3, 3, 1, 1, 2, 2))]
    kept0, a0, b0, c0 = partial(
        base, (block, x0, up1, up2, down1, down2, far1, far2), layout0, weight, weight_other, up_own, up_other, down3
    )
    small_other = across(small, "xl", 1)
    up4, down4, kept0, a0, b0, c0, small, small_other = phase(up4, down4, kept0, a0, b0, c0, small, small_other)
    small = small + small_other

    up5, down5 = ahead(up4[:q], "z", 1), ahead(down4[q:], "z", 3)
    a0, c0 = ahead(a0, "y", 1), ahead(c0, "y", 3)
    low48 = jnp.concatenate(pieces3(scaling * small[:rank]), axis=0)
    proj48 = jnp.concatenate(pieces3(scaling * small[rank:]), axis=0)

    def three(left, right):
        out = jnp.dot(left, right, preferred_element_type=jnp.float32)
        return out[:rank] + (out[rank : 2 * rank] + out[2 * rank :])

    parts = jnp.concatenate([three(low48, inputs), three(proj48, cotangent)], axis=1)
    parts_other = across(parts, "xh", 1)
    up5, down5, a0, c0, b0, parts, parts_other = phase(up5, down5, a0, c0, b0, parts, parts_other)
    parts = parts + parts_other

    layout1 = [
        (0, p, q, 0, 0),
        (1, 0, q, 0, q),
        (2, 0, 2 * q, 3, 0),
        (3, 0, 2 * q, 1, 0),
        (4, 0, q, 2, 0),
        (5, 0, q, 2, q),
    ]

    def half_of_sums(which, *given):
        return partial_half(
            which, base, (block, x1, up4, down4, up5, down5), layout1, weight, weight_other, given, down3
        )

    b0 = ahead(b0, "y", 2)
    kept1, a1, b1, c1, factors = half_of_sums(0, up_own, up_other)
    kept1, a1, b1, c1, b0, parts, block, factors = phase(kept1, a1, b1, c1, b0, parts, block, factors)

    a1, c1, b1 = ahead(a1, "y", 1), ahead(c1, "y", 3), ahead(b1, "y", 2)
    parts_other = across(parts, "z", 1)
    kept2, a2, b2, c2, _ = half_of_sums(1, factors)
    kept2, a2, b2, c2, a1, c1, b1, b0, parts_other = phase(kept2, a2, b2, c2, a1, c1, b1, b0, parts_other)
    parts = parts + parts_other

    a2, c2, b2 = ahead(a2, "y", 1), ahead(c2, "y", 3), ahead(b2, "y", 2)
    parts_other = across(parts, "z", 2)
    keep0, keep1, send1 = fold(swap, (kept0, a0, c0, b0), (kept1, a1, c1, b1))
    a2, c2, b2, keep0, keep1, send1, parts_other = phase(a2, c2, b2, keep0, keep1, send1, parts_other)

    got1 = across(send1, "xl", 1)
    keep2, send2 = fold(swap, (kept2, a2, c2, b2))
    got2 = across(send2, "xl", 1)
    parts = after(parts, send2) + parts_other
    grad_a = parts[:, :width_row_block].T
    grad_b = parts[:, width_row_block:]
    got1, got2, grad_a, grad_b = phase(got1, got2, grad_a, grad_b)
    grad_input = finish(keep0, keep1, got1, keep2, got2).T
    return grad_input, grad_a, grad_b


def solution(mesh):
    fine = Mesh(mesh.devices.reshape(SIZES), AXES)
    in_specs = (P(COL, ROW), P(COL, ROW), P(COL, ROW), P(), P())
    out_specs = (P(ROW, COL), P(ROW, None), P(None, ROW))
    return jax.shard_map(on_device, mesh=fine, in_specs=in_specs, out_specs=out_specs, check_vma=False)
```
